32 devices in a mesh: page: 8 (over y, x, core), band: 4 (over z).
Axes of the slice: x: 2, y: 2, z: 4, core: 2. Of those that a mesh axis runs over, the one named last changes fastest.
Arguments:
- hidden_in: bfloat16 [10240, 768], P(('page', 'band')), may hold values from -6 to 6
- lengths: int32 [8, 40], P('page'), may hold values from 1 to 512, 1280 in all within a row
- permutation: int32 [8, 1280], P('page', 'band'), may hold values from 0 to 1279, as said below
- query_weight: float32 [768, 768], P(('page', 'band')), may hold values from -0.21875 to 0.21875
- query_bias: float32 [768], P(('page', 'band')), may hold values from -3 to 3
- key_weight: float32 [768, 768], P(('page', 'band')), may hold values from -0.21875 to 0.21875
- value_weight: float32 [768, 768], P(('page', 'band')), may hold values from -0.21875 to 0.21875
- value_bias: float32 [768], P(('page', 'band')), may hold values from -3 to 3
- mix_weight: float32 [768, 768], P(('page', 'band')), may hold values from -0.875 to 0.875
- mix_bias: float32 [768], P(('page', 'band')), may hold values from -3 to 3
- first_gain: float32 [768], P(('page', 'band')), may hold values from 0.4 to 1.6
- first_shift: float32 [768], P(('page', 'band')), may hold values from -3 to 3
- expand_weight: float32 [768, 3072], P(('page', 'band')), may hold values from -0.21875 to 0.21875
- expand_bias: float32 [3072], P(('page', 'band')), may hold values from -3 to 3
- contract_weight: float32 [3072, 768], P(('page', 'band')), may hold values from -0.21875 to 0.21875
- contract_bias: float32 [768], P(('page', 'band')), may hold values from -3 to 3
- second_gain: float32 [768], P(('page', 'band')), may hold values from 0.4 to 1.6
- second_shift: float32 [768], P(('page', 'band')), may hold values from -3 to 3
- cotangent: bfloat16 [10240, 768], P(('page', 'band')), may hold values from -6 to 6
Outputs:
- layer_output: bfloat16 [10240, 768], P(('page', 'band'))
- input_gradient: bfloat16 [10240, 768], P(('page', 'band'))
- query_weight_gradient: float32 [768, 768], P(('page', 'band'))
- query_bias_gradient: float32 [768], P(('page', 'band'))
- key_weight_gradient: float32 [768, 768], P(('page', 'band'))
- value_weight_gradient: float32 [768, 768], P(('page', 'band'))
- value_bias_gradient: float32 [768], P(('page', 'band'))
- mix_weight_gradient: float32 [768, 768], P(('page', 'band'))
- mix_bias_gradient: float32 [768], P(('page', 'band'))
- first_gain_gradient: float32 [768], P(('page', 'band'))
- first_shift_gradient: float32 [768], P(('page', 'band'))
- expand_weight_gradient: float32 [768, 3072], P(('page', 'band'))
- expand_bias_gradient: float32 [3072], P(('page', 'band'))
- contract_weight_gradient: float32 [3072, 768], P(('page', 'band'))
- contract_bias_gradient: float32 [768], P(('page', 'band'))
- second_gain_gradient: float32 [768], P(('page', 'band'))
- second_shift_gradient: float32 [768], P(('page', 'band'))
The draws below stay inside these ranges and needn't reach their ends.
Inputs may be any that keep to these rules, and one draw needn't show every extreme that they name: Each row lists the 40 document lengths of one page group; they sum to 1280, and the longest is exactly 512. Each row is a permutation of 0 .. 1279; the positions k * 1280 // 320 to (k + 1) * 1280 // 320 - 1 lie in slots of different bands, one on each.
All inputs are finite; a program needn't handle non-finite values.
Results may differ from the reference program's by a relative error of at most 0.017.
Values may be sent and summed in bfloat16 or wider, within the bound.
No kernel may reach another device: no remote copies, remote signals or barrier semaphores. Data moves between devices by JAX's collectives and lax.ppermute only.
A program may use at most 192 MiB of HBM per device.

```python
import math
import jax
import jax.numpy as jnp
import numpy as np
from jax import lax

D = 768
FF = 3072
HEADS = 12
HEAD_DIM = 64
TOK_DEV = 320
PAGE_LEN = 512
GROUP = 1280
PAGES = 8
TOKENS = 10240
DOCS = 40


def slot_positions(group_key):
    band_count = GROUP // TOK_DEV
    row_order = jax.random.permutation(jax.random.fold_in(group_key, 1), TOK_DEV)
    band_keys = jax.random.split(jax.random.fold_in(group_key, 2), TOK_DEV)
    band_order = jax.vmap(lambda item_key: jax.random.permutation(item_key, band_count))(band_keys)
    positions = row_order[:, None] * band_count + band_order
    return jnp.transpose(positions).reshape(GROUP)


def draw_permutation(key, part):
    key = jax.random.fold_in(key, 7)
    return jax.vmap(slot_positions)(jax.random.split(key, PAGES)).astype(jnp.int32)


def level_of(rng, dims, shards, low, largest):
    factor_of, own = 1.0, jax.random.fold_in(rng, 6)
    for axis_at, blocks in shards:
        heights = jnp.exp(jax.random.uniform(jax.random.fold_in(own, axis_at), (blocks,), jnp.float32, low / len(shards), largest / len(shards)))
        factor_of = factor_of * jnp.repeat(heights, dims[axis_at] // blocks).reshape([-1 if axis == axis_at else 1 for axis in range(len(dims))])
    return factor_of


def profile(amount, total, limit, slope):
    weights = [(1 << 20) // math.isqrt(rank ** slope) + 1 for rank in range(2, amount + 1)]
    rest, holding = total - limit - (amount - 1), [1] * (amount - 1)
    while rest > 0:
        movable = [i for i in range(amount - 1) if holding[i] < limit]
        whole, remaining = sum([weights[i] for i in movable]), rest
        for i in movable:
            extra = min(limit - holding[i], max(1, remaining * weights[i] // whole), rest)
            holding[i] = holding[i] + extra
            rest = rest - extra
    return np.array([limit] + holding)


def uneven_parts(stream_key, count, total, most, slope):
    if count == 2:
        one = jax.random.randint(stream_key, (), max(1, total - most), min(most, total - 1) + 1)
        return jnp.stack([one, total - one])
    sizes = jnp.asarray(profile(count, total, most, slope), jnp.int32)
    pairs = (count - 1) // 2
    source_of, sink = sizes[1:1 + 2 * pairs:2], sizes[2:2 + 2 * pairs:2]
    margin = jnp.minimum(source_of - 1, most - sink)
    moved = jax.random.randint(jax.random.fold_in(stream_key, 1), (pairs,), 0, 1 << 20) % (margin + 1)
    sizes = sizes.at[1:1 + 2 * pairs:2].set(source_of - moved).at[2:2 + 2 * pairs:2].set(sink + moved)
    return sizes[jax.random.permutation(jax.random.fold_in(stream_key, 2), count)]


def gaussian(stream_key, shape, spread, reach, cuts=(), held_as=jnp.bfloat16):
    level = level_of(stream_key, shape, cuts, -0.22, 0.18) if cuts else 1.0
    values = jax.random.normal(stream_key, shape, jnp.float32) * spread * level
    return jnp.minimum(jnp.maximum(values, -reach), reach).astype(held_as)


def setup_inputs(seed: int = 0) -> dict:
    keys = jax.random.split(jax.random.key(seed), 20)
    return {
        "hidden_in": gaussian(keys[0], (TOKENS, D), 1.0, 6.0, ((0, 32),)),
        "lengths": jax.vmap(lambda own: uneven_parts(own, DOCS, GROUP, PAGE_LEN, 2))(jax.random.split(keys[1], PAGES)).reshape((PAGES, DOCS)).astype(jnp.int32),
        "permutation": draw_permutation(jax.random.fold_in(keys[19], 71), 0),
        "query_weight": gaussian(keys[3], (D, D), D ** -0.5, 0.21875, ((0, 32),), jnp.float32),
        "query_bias": gaussian(keys[4], (D,), 0.5, 3.0, ((0, 32),), jnp.float32),
        "key_weight": gaussian(keys[5], (D, D), D ** -0.5, 0.21875, ((0, 32),), jnp.float32),
        "value_weight": gaussian(keys[6], (D, D), D ** -0.5, 0.21875, ((0, 32),), jnp.float32),
        "value_bias": gaussian(keys[7], (D,), 0.5, 3.0, ((0, 32),), jnp.float32),
        "mix_weight": gaussian(keys[8], (D, D), (D // 16) ** -0.5, 0.875, ((0, 32),), jnp.float32),
        "mix_bias": gaussian(keys[9], (D,), 0.5, 3.0, ((0, 32),), jnp.float32),
        "first_gain": jnp.clip(1.0 + 0.12 * jax.random.normal(keys[10], (D,), jnp.float32), 0.4, 1.6),
        "first_shift": gaussian(keys[11], (D,), 0.5, 3.0, ((0, 32),), jnp.float32),
        "expand_weight": gaussian(keys[12], (D, FF), D ** -0.5, 0.21875, ((0, 32),), jnp.float32),
        "expand_bias": gaussian(keys[13], (FF,), 0.5, 3.0, ((0, 32),), jnp.float32),
        "contract_weight": gaussian(keys[14], (FF, D), (FF // 4) ** -0.5, 0.21875, ((0, 32),), jnp.float32),
        "contract_bias": gaussian(keys[15], (D,), 0.5, 3.0, ((0, 32),), jnp.float32),
        "second_gain": jnp.clip(1.0 + 0.12 * jax.random.normal(keys[16], (D,), jnp.float32), 0.4, 1.6),
        "second_shift": gaussian(keys[17], (D,), 0.5, 3.0, ((0, 32),), jnp.float32),
        "cotangent": gaussian(keys[18], (TOKENS, D), 1.0, 6.0, ((0, 32),)),
    }


EPSILON = 1e-12
PRECISE = lax.Precision.HIGHEST

@jax.custom_vjp
def low(v):
    return lax.optimization_barrier(v.astype(jnp.bfloat16)).astype(jnp.float32)

@jax.custom_vjp
def low_back(v):
    return v

def low_keep(v):
    return (low(v), None)

def low_pass(kept, grad):
    return (grad,)

def back_keep(v):
    return (v, None)

def back_low(kept, grad):
    return (low(grad),)
low.defvjp(low_keep, low_pass)
low_back.defvjp(back_keep, back_low)

def product(left, right):
    return jnp.dot(left, right, precision=PRECISE, preferred_element_type=jnp.float32)

def exact_gelu(values):
    return jax.nn.gelu(values, approximate=False)

def layer_norm(inputs, scale_gain, shift_bias):
    centred = inputs - lax.optimization_barrier(jnp.mean(inputs, axis=-1, keepdims=True))
    variance = lax.optimization_barrier(jnp.mean(centred * centred, axis=-1, keepdims=True))
    return centred * lax.rsqrt(variance + EPSILON) * scale_gain + shift_bias

def attend_group(block):
    query_part, key_part, value_part, group_docs = block
    same_doc = group_docs[:, None] == group_docs[None, :]
    raw_scores = low_back(jnp.einsum('qhd,khd->hqk', query_part, key_part, precision=PRECISE))
    scores = jnp.where(same_doc[None], raw_scores * HEAD_DIM ** (-0.5), -1e+30)
    row_peak = lax.optimization_barrier(jnp.max(scores, axis=-1, keepdims=True))
    unscaled = jnp.exp(scores - row_peak)
    attention_weights = low(unscaled / lax.optimization_barrier(jnp.sum(unscaled, axis=-1, keepdims=True)))
    return jnp.einsum('hqk,khd->qhd', attention_weights, value_part, precision=PRECISE)

def forward(hidden, params, group_docs):
    w_query, b_query, w_key, w_value, b_value, w_mix, b_mix, gain_one, shift_one, w_expand, b_expand, w_contract, b_contract, gain_two, shift_two = tuple((low(item) for item in params))
    query = low_back(low(product(hidden, w_query) + b_query))
    key_rows = low_back(low(product(hidden, w_key)))
    value_rows = low_back(low(product(hidden, w_value) + b_value))
    shaped = (PAGES, GROUP, HEADS, HEAD_DIM)
    attended = lax.map(jax.checkpoint(attend_group), (query.reshape(shaped), key_rows.reshape(shaped), value_rows.reshape(shaped), group_docs))
    attended = low_back(low(attended.reshape(TOKENS, D)))
    mix_out = low_back(product(attended, w_mix) + b_mix)
    first = layer_norm(hidden + mix_out, gain_one, shift_one)
    expanded = low_back(product(low(first), w_expand) + b_expand)
    activated = low(exact_gelu(expanded))
    contracted = low_back(product(activated, w_contract) + b_contract)
    return layer_norm(first + contracted, gain_two, shift_two)

def reference(hidden_in, lengths, permutation, query_weight, query_bias, key_weight, value_weight, value_bias, mix_weight, mix_bias, first_gain, first_shift, expand_weight, expand_bias, contract_weight, contract_bias, second_gain, second_shift, cotangent):
    ends = jnp.cumsum(lengths.astype(jnp.int32), axis=1)
    group_docs = lax.optimization_barrier(jnp.sum((permutation.astype(jnp.int32)[:, :, None] >= ends[:, None, :]).astype(jnp.int32), axis=2)).astype(jnp.int32)
    params = (query_weight, query_bias, key_weight, value_weight, value_bias, mix_weight, mix_bias, first_gain, first_shift, expand_weight, expand_bias, contract_weight, contract_bias, second_gain, second_shift)
    params = tuple((item.astype(jnp.float32) for item in params))
    hidden = hidden_in.astype(jnp.float32)
    result, pullback = jax.vjp(lambda rows, weights: forward(rows, weights, group_docs), hidden, params)
    grad_hidden, grads = pullback(cotangent.astype(jnp.float32))
    return (result.astype(jnp.bfloat16), grad_hidden.astype(jnp.bfloat16), grads[0], grads[1], grads[2], grads[3], grads[4], grads[5], grads[6], grads[7], grads[8], grads[9], grads[10], grads[11], grads[12], grads[13], grads[14])
```

```python
import functools
import itertools
import math

import jax
import jax.numpy as jnp
from jax import lax
from jax.experimental import pallas as pl
from jax.experimental.pallas import tpu as pltpu
from jax.sharding import PartitionSpec as P

HEAD_DIM = 64
PAIR = 2 * HEAD_DIM
EPSILON = 1e-12
AXES = ("page", "band")
SLAB = 128
TAIL = 16
BF16, F32 = jnp.bfloat16, jnp.float32
VMEM_LIMIT = 56 * 2**20


def dot(left, right):
    return lax.dot_general(left, right, (((1,), (0,)), ((), ())), preferred_element_type=F32)


def times_transposed(left, right):
    return lax.dot_general(left, right, (((1,), (1,)), ((), ())), preferred_element_type=F32)


def outer_sum(left, right):
    return lax.dot_general(left, right, (((0,), (0,)), ((), ())), preferred_element_type=F32)


class Grid:
    def __init__(self, pages, bands):
        self.side = math.isqrt(pages // 2)
        assert self.side * self.side * 2 == pages
        self.bands = bands
        self.devices = pages * bands
        self.quads = self.side * self.side

    def linear(self, i, j, c, z):
        return ((i * self.side + j) * 2 + c) * self.bands + z

    def permute(self, array, move):
        side, bands = self.side, self.bands
        pairs = []
        for i, j, c, z in itertools.product(range(side), range(side), range(2), range(bands)):
            ti, tj, tc, tz = move(i, j, c, z)
            pairs.append((self.linear(i, j, c, z), self.linear(ti % side, tj % side, tc, tz % bands)))
        return lax.ppermute(array, AXES, pairs)

    def along_z(self, array, step):
        return self.permute(array, lambda i, j, c, z: (i, j, c, z + step))

    def near(self, array, step):
        return self.permute(
            array, lambda i, j, c, z: (i, j + step, c, z) if c == 0 else (i + step, j, c, z)
        )

    def far(self, array, step):
        return self.permute(
            array, lambda i, j, c, z: (i + step, j, c, z) if c == 0 else (i, j + step, c, z)
        )

    def across(self, array):
        return self.permute(array, lambda i, j, c, z: (i, j, 1 - c, z))

    def place(self):
        page, z = lax.axis_index("page"), lax.axis_index("band")
        return page // (2 * self.side), (page // 2) % self.side, page % 2, z


def gather_rows(grid, shard):
    rows, width = shard.shape
    i, j, c, z = grid.place()
    block = jnp.zeros((grid.bands, rows, width), shard.dtype)
    for step in range(grid.bands):
        piece = shard if step == 0 else grid.along_z(shard, step)
        block = lax.dynamic_update_slice(block, piece[None], ((z - step) % grid.bands, 0, 0))
    tall = grid.bands * rows
    block = block.reshape(tall, width)
    near = [block] + [grid.near(block, step) for step in range(1, grid.side)]
    near_all = jnp.stack(near)
    far = [near_all] + [grid.far(near_all, step) for step in range(1, grid.side)]
    own = [far[a][b] for a in range(grid.side) for b in range(grid.side)]
    sent = [near_all] + far[1:]
    other = [grid.across(item) for item in sent]
    other = [other[a][b] for a in range(grid.side) for b in range(grid.side)]
    whole = jnp.zeros((grid.quads * 2, tall, width), shard.dtype)
    for core, blocks in ((c, own), (1 - c, other)):
        for a in range(grid.side):
            for b in range(grid.side):
                di = jnp.where(core == 0, a, b)
                dj = jnp.where(core == 0, b, a)
                index = (((i - di) % grid.side) * grid.side + (j - dj) % grid.side) * 2 + core
                whole = lax.dynamic_update_slice(whole, blocks[a * grid.side + b][None], (index, 0, 0))
    return whole.reshape(grid.devices * rows, width)


def relative(grid, full):
    rows = full.shape[0] // grid.devices
    i, j, c, z = grid.place()
    blocks = full.reshape(grid.quads * 2, grid.bands, rows, full.shape[1])
    cores = []
    for d in range(2):
        core = (c + d) % 2
        fars = []
        for a in range(grid.side):
            nears = []
            for b in range(grid.side):
                di = jnp.where(core == 0, a, b)
                dj = jnp.where(core == 0, b, a)
                index = (((i + di) % grid.side) * grid.side + (j + dj) % grid.side) * 2 + core
                nears.append(lax.dynamic_index_in_dim(blocks, index, 0, False))
            fars.append(nears)
        cores.append(fars)
    return cores


def scatter_sum(grid, full):
    side = grid.side
    z = lax.axis_index("band")
    keep, send = relative(grid, full)
    send = jnp.stack([jnp.stack(row) for row in send])
    got = grid.across(send)
    total = [[keep[a][b].astype(F32) + got[a, b].astype(F32) for b in range(side)] for a in range(side)]
    for a in range(1, side):
        got = grid.far(jnp.stack(total[a]).astype(BF16), a)
        for b in range(side):
            total[0][b] = total[0][b] + got[b].astype(F32)
    own = total[0][0]
    for b in range(1, side):
        own = own + grid.near(total[0][b].astype(BF16), b).astype(F32)
    result = lax.dynamic_index_in_dim(own, z, 0, False)
    for step in range(1, grid.bands):
        part = lax.dynamic_index_in_dim(own, (z + step) % grid.bands, 0, False).astype(BF16)
        result = result + grid.along_z(part, step).astype(F32)
    return result


def head_mask(rows, head):
    lanes = lax.broadcasted_iota(jnp.int32, (rows, PAIR), 1)
    return (lanes // HEAD_DIM) == head


def attend_kernel(pieces, *refs):
    hidden = refs[:pieces]
    wq, wk, wv, vec, own_doc, all_doc = refs[pieces : pieces + 6]
    q_out, k_out, v_out, att_out, log_out, bias = refs[pieces + 6 :]
    tokens = q_out.shape[0]
    keys = k_out.shape[0]

    @pl.when(pl.program_id(0) == 0)
    def _():
        bias[...] = jnp.where(own_doc[...] == all_doc[...], 0.0, -1e30).astype(F32)

    q_out[...] = (dot(hidden[0][0:tokens, :], wq[...]) + vec[0:1, :]).astype(BF16)
    for p in range(pieces):
        rows = slice(p * tokens, (p + 1) * tokens)
        part = hidden[p][0:tokens, :]
        k_out[rows, :] = dot(part, wk[...]).astype(BF16)
        v_out[rows, :] = (dot(part, wv[...]) + vec[1:2, :]).astype(BF16)
    lane = lax.broadcasted_iota(jnp.int32, (tokens, 128), 1)
    logs = jnp.zeros((tokens, 128), F32)
    ones = jnp.ones((keys, PAIR), BF16)
    for pair in range(q_out.shape[1] // PAIR):
        cols = slice(pair * PAIR, (pair + 1) * PAIR)
        query = q_out[:, cols]
        key = k_out[:, cols]
        value = jnp.concatenate([v_out[:, cols], ones], axis=1)
        outs = []
        for head in range(2):
            picked = jnp.where(head_mask(tokens, head), query * HEAD_DIM**-0.5, 0).astype(BF16)
            scores = times_transposed(picked, key) + bias[...]
            peak = jnp.max(scores, axis=1, keepdims=True)
            weights = jnp.exp(scores - peak).astype(BF16)
            both = dot(weights, value)
            outs.append(both[:, :PAIR] / both[:, PAIR:])
            total = peak + jnp.log(both[:, PAIR:])
            logs = jnp.where(lane == pair * 2 + head, total, logs)
        att_out[:, cols] = jnp.where(head_mask(tokens, 0), outs[0], outs[1]).astype(BF16)
    log_out[...] = logs[None]


def attend(hidden, weights, vec, own_doc, all_doc):
    pieces = len(hidden)
    tokens, width = hidden[0].shape
    keys = pieces * tokens
    step = 256
    groups = width // step
    column = lambda offset: pl.BlockSpec((width, step), lambda g, o=offset: (0, o * groups + g))
    whole = lambda shape: pl.BlockSpec(shape, lambda g: (0, 0))
    tall = lambda rows: pl.BlockSpec((rows, step), lambda g: (0, g))
    return pl.pallas_call(
        functools.partial(attend_kernel, pieces),
        grid=(groups,),
        in_specs=[whole(item.shape) for item in hidden]
        + [column(0), column(1), column(2), tall(8), whole(own_doc.shape), whole(all_doc.shape)],
        out_specs=[
            tall(tokens),
            tall(keys),
            tall(keys),
            tall(tokens),
            pl.BlockSpec((1, tokens, 128), lambda g: (g, 0, 0)),
        ],
        out_shape=[
            jax.ShapeDtypeStruct((tokens, width), BF16),
            jax.ShapeDtypeStruct((keys, width), BF16),
            jax.ShapeDtypeStruct((keys, width), BF16),
            jax.ShapeDtypeStruct((tokens, width), BF16),
            jax.ShapeDtypeStruct((groups, tokens, 128), F32),
        ],
        scratch_shapes=[pltpu.VMEM((tokens, keys), F32)],
        compiler_params=pltpu.CompilerParams(vmem_limit_bytes=VMEM_LIMIT),
        cost_estimate=pl.CostEstimate(
            flops=2 * keys * width * width * 3, bytes_accessed=16 * 2**20, transcendentals=0
        ),
        name="attend",
    )(*hidden, weights, weights, weights, vec, own_doc, all_doc)


def attend_back_kernel(q, k, v, grad, att, logs, own_doc, all_doc, dq_out, dk_out, dv_out, bias):
    tokens = q.shape[0]
    pair = pl.program_id(0)

    @pl.when(pair == 0)
    def _():
        bias[...] = jnp.where(own_doc[...] == all_doc[...], 0.0, -1e30).astype(F32)

    lane = lax.broadcasted_iota(jnp.int32, (tokens, 128), 1)
    key, value = k[...], v[...]
    product = grad[...].astype(F32) * att[...].astype(F32)
    dq, dk, dv = [], 0.0, 0.0
    for head in range(2):
        mask = head_mask(tokens, head)
        query = jnp.where(mask, q[...] * HEAD_DIM**-0.5, 0).astype(BF16)
        part = jnp.where(mask, grad[...], 0).astype(BF16)
        slot = (pair % 2) * 2 + head
        log_total = jnp.sum(jnp.where(lane == slot, logs[0], 0.0), axis=1, keepdims=True)
        inner = jnp.sum(jnp.where(mask, product, 0.0), axis=1, keepdims=True)
        weights = jnp.exp(times_transposed(query, key) + bias[...] - log_total)
        back = (weights * (times_transposed(part, value) - inner)).astype(BF16)
        dq.append(dot(back, key) * HEAD_DIM**-0.5)
        dk = dk + outer_sum(back, query)
        dv = dv + outer_sum(weights.astype(BF16), part)
    dq_out[...] = jnp.where(head_mask(tokens, 0), dq[0], dq[1]).astype(BF16)
    dk_out[...] = dk.astype(BF16)
    dv_out[...] = dv.astype(BF16)


def attend_back(q, k, v, grad, att, logs, own_doc, all_doc):
    tokens, width = q.shape
    keys = k.shape[0]
    short = pl.BlockSpec((tokens, PAIR), lambda g: (0, g))
    tall = pl.BlockSpec((keys, PAIR), lambda g: (0, g))
    whole = lambda shape: pl.BlockSpec(shape, lambda g: (0, 0))
    return pl.pallas_call(
        attend_back_kernel,
        grid=(width // PAIR,),
        in_specs=[
            short,
            tall,
            tall,
            short,
            short,
            pl.BlockSpec((1, tokens, 128), lambda g: (g // 2, 0, 0)),
            whole(own_doc.shape),
            whole(all_doc.shape),
        ],
        out_specs=[short, tall, tall],
        out_shape=[
            jax.ShapeDtypeStruct((tokens, width), BF16),
            jax.ShapeDtypeStruct((keys, width), BF16),
            jax.ShapeDtypeStruct((keys, width), BF16),
        ],
        scratch_shapes=[pltpu.VMEM((tokens, keys), F32)],
        compiler_params=pltpu.CompilerParams(vmem_limit_bytes=VMEM_LIMIT),
        cost_estimate=pl.CostEstimate(
            flops=2 * keys * width * width * 4, bytes_accessed=16 * 2**20, transcendentals=0
        ),
        name="attend_back",
    )(q, k, v, grad, att, logs, own_doc, all_doc)


def layer_norm(inputs, scale_gain, shift_bias):
    centred = inputs - jnp.mean(inputs, axis=-1, keepdims=True)
    variance = jnp.mean(centred * centred, axis=-1, keepdims=True)
    inverse = lax.rsqrt(variance + EPSILON)
    normed = centred * inverse
    return normed * scale_gain + shift_bias, normed, inverse


def norm_back(grad_out, normed, inverse, scale_gain):
    grad_normed = grad_out * scale_gain
    inner = (
        grad_normed
        - jnp.mean(grad_normed, axis=-1, keepdims=True)
        - normed * jnp.mean(grad_normed * normed, axis=-1, keepdims=True)
    )
    return inner * inverse, jnp.sum(grad_out * normed, axis=0), jnp.sum(grad_out, axis=0)


def per_device(
    grid,
    hidden_in,
    lengths,
    permutation,
    query_weight,
    query_bias,
    key_weight,
    value_weight,
    value_bias,
    mix_weight,
    mix_bias,
    first_gain,
    first_shift,
    expand_weight,
    expand_bias,
    contract_weight,
    contract_bias,
    second_gain,
    second_shift,
    cotangent,
):
    tokens, width = hidden_in.shape
    wide = contract_weight.shape[0] * grid.devices
    rows = query_weight.shape[0]
    bands = grid.bands

    ends = jnp.cumsum(lengths[0])
    docs = jnp.sum((permutation[0][:, None] >= ends[None, :]).astype(jnp.int32), axis=1)
    own_doc = docs.astype(F32)[:, None]
    vectors = [query_bias, value_bias, mix_bias, first_gain, first_shift, contract_bias, second_gain, second_shift]
    slab = jnp.concatenate(
        [jnp.stack(vectors, axis=1), expand_bias.reshape(rows, wide // width)], axis=1
    )
    slab = jnp.pad(slab, ((0, 0), (0, SLAB - slab.shape[1])))
    shard_a = jnp.concatenate([query_weight, key_weight, value_weight, slab], axis=1).astype(BF16)
    shard_b = jnp.concatenate([mix_weight, expand_weight], axis=1).astype(BF16)
    shard_c = contract_weight.astype(BF16)
    marks = jnp.pad(docs.astype(BF16)[None], ((0, TAIL - 1), (0, width - tokens)))
    message = jnp.concatenate([hidden_in, marks])

    full_a = gather_rows(grid, shard_a)
    others = [grid.along_z(message, step) for step in range(1, bands)]
    full_b = gather_rows(grid, shard_b)
    full_c = gather_rows(grid, shard_c)

    hidden = [hidden_in] + [item[:tokens] for item in others]
    all_doc = jnp.concatenate(
        [docs.astype(F32)[None]] + [item[tokens : tokens + 1, :tokens].astype(F32) for item in others], axis=1
    )
    slabs = full_a[:, 3 * width :].astype(F32)
    vec = jnp.transpose(slabs[:, :8])
    b_expand = slabs[:, 8 : 8 + wide // width].reshape(wide)

    q, k, v, attended, logs = attend(hidden, full_a, vec, own_doc, all_doc)

    w_mix, w_expand = full_b[:, :width], full_b[:, width:]
    _, _, b_mix, gain_one, shift_one, b_contract, gain_two, shift_two = [vec[n] for n in range(8)]
    first, first_normed, first_inverse = layer_norm(
        hidden_in.astype(F32) + (dot(attended, w_mix) + b_mix), gain_one, shift_one
    )
    first_low = first.astype(BF16)
    expanded = dot(first_low, w_expand) + b_expand
    chance = 0.5 * (1.0 + lax.erf(expanded * (0.5**0.5)))
    density = jnp.exp(-0.5 * expanded * expanded) * ((2.0 * math.pi) ** -0.5)
    activated = (expanded * chance).astype(BF16)
    slope = chance + expanded * density
    contracted = dot(activated, full_c) + b_contract
    result, second_normed, second_inverse = layer_norm(first + contracted, gain_two, shift_two)
    grad_second, d_gain_two, d_shift_two = norm_back(
        cotangent.astype(F32), second_normed, second_inverse, gain_two
    )
    contract_low = grad_second.astype(BF16)
    d_contract = scatter_sum(grid, outer_sum(activated, contract_low).astype(BF16))
    d_b_contract = jnp.sum(contract_low.astype(F32), axis=0)
    expanded_low = (times_transposed(contract_low, full_c) * slope).astype(BF16)
    d_b_expand = jnp.sum(expanded_low.astype(F32), axis=0)
    grad_first = grad_second + times_transposed(expanded_low, w_expand)
    grad_first_sum, d_gain_one, d_shift_one = norm_back(grad_first, first_normed, first_inverse, gain_one)
    mixed_low = grad_first_sum.astype(BF16)
    d_b_mix = jnp.sum(mixed_low.astype(F32), axis=0)
    d_b = jnp.concatenate([outer_sum(attended, mixed_low), outer_sum(first_low, expanded_low)], axis=1)
    d_b = scatter_sum(grid, d_b.astype(BF16))
    attended_back = times_transposed(mixed_low, w_mix).astype(BF16)

    dq, dk, dv = attend_back(q, k, v, attended_back, attended, logs, own_doc, all_doc)
    w_query, w_key, w_value = [full_a[:, n * width : (n + 1) * width] for n in range(3)]
    back = times_transposed(dk, w_key) + times_transposed(dv, w_value)
    grad_input = grad_first_sum + times_transposed(dq, w_query) + back[:tokens]
    for step in range(1, bands):
        part = back[step * tokens : (step + 1) * tokens].astype(BF16)
        grad_input = grad_input + grid.along_z(part, -step).astype(F32)

    every = jnp.concatenate(hidden)
    column = lambda item: jnp.sum(item.astype(F32), axis=0)
    d_vec = jnp.stack(
        [column(dq), column(dv), d_b_mix, d_gain_one, d_shift_one, d_b_contract, d_gain_two, d_shift_two]
    )
    d_slab = jnp.concatenate([jnp.transpose(d_vec), d_b_expand.reshape(width, wide // width)], axis=1)
    d_slab = jnp.pad(d_slab, ((0, 0), (0, SLAB - d_slab.shape[1])))
    d_a = jnp.concatenate(
        [
            outer_sum(hidden_in, dq),
            outer_sum(every, dk),
            outer_sum(every, dv),
            d_slab,
        ],
        axis=1,
    )
    d_a = scatter_sum(grid, d_a.astype(BF16))
    slab = d_a[:, 3 * width :]
    small = [slab[:, n] for n in range(8)]
    return (
        result.astype(BF16),
        grad_input.astype(BF16),
        d_a[:, :width],
        small[0],
        d_a[:, width : 2 * width],
        d_a[:, 2 * width : 3 * width],
        small[1],
        d_b[:, :width],
        small[2],
        small[3],
        small[4],
        d_b[:, width:],
        slab[:, 8 : 8 + wide // width].reshape(-1),
        d_contract,
        small[5],
        small[6],
        small[7],
    )


def solution(mesh):
    grid = Grid(mesh.shape["page"], mesh.shape["band"])
    matrix, vector = P(AXES, None), P(AXES)
    parameters = (
        matrix,
        vector,
        matrix,
        matrix,
        vector,
        matrix,
        vector,
        vector,
        vector,
        matrix,
        vector,
        matrix,
        vector,
        vector,
        vector,
    )
    return jax.shard_map(
        functools.partial(per_device, grid),
        mesh=mesh,
        in_specs=(matrix, P("page", None), P("page", "band")) + parameters + (matrix,),
        out_specs=(matrix, matrix) + parameters,
        check_vma=False,
    )
```

```python
import functools
import itertools
import math

import jax
import jax.numpy as jnp
from jax import lax
from jax.experimental import pallas as pl
from jax.experimental.pallas import tpu as pltpu
from jax.sharding import PartitionSpec as P

HEAD_DIM = 64
PAIR = 2 * HEAD_DIM
EPSILON = 1e-12
AXES = ("page", "band")
SLAB = 256
BF16, F32 = jnp.bfloat16, jnp.float32
VMEM_LIMIT = 56 * 2**20
CHEAP = pl.CostEstimate(flops=1024, bytes_accessed=1024, transcendentals=0)


def dot(left, right):
    return lax.dot_general(left, right, (((1,), (0,)), ((), ())), preferred_element_type=F32)


def times_transposed(left, right):
    return lax.dot_general(left, right, (((1,), (1,)), ((), ())), preferred_element_type=F32)


def outer_sum(left, right):
    return lax.dot_general(left, right, (((0,), (0,)), ((), ())), preferred_element_type=F32)


class Grid:
    def __init__(self, pages, bands):
        self.side = math.isqrt(pages // 2)
        assert self.side * self.side * 2 == pages
        self.bands = bands
        self.devices = pages * bands
        self.quads = self.side * self.side

    def linear(self, i, j, c, z):
        return ((i * self.side + j) * 2 + c) * self.bands + z

    def permute(self, array, move):
        side, bands = self.side, self.bands
        pairs = []
        for i, j, c, z in itertools.product(range(side), range(side), range(2), range(bands)):
            ti, tj, tc, tz = move(i, j, c, z)
            pairs.append((self.linear(i, j, c, z), self.linear(ti % side, tj % side, tc, tz % bands)))
        return lax.ppermute(array, AXES, pairs)

    def along_z(self, array, step):
        return self.permute(array, lambda i, j, c, z: (i, j, c, z + step))

    def near(self, array, step):
        return self.permute(
            array, lambda i, j, c, z: (i, j + step, c, z) if c == 0 else (i + step, j, c, z)
        )

    def far(self, array, step):
        return self.permute(
            array, lambda i, j, c, z: (i + step, j, c, z) if c == 0 else (i, j + step, c, z)
        )

    def across(self, array):
        return self.permute(array, lambda i, j, c, z: (i, j, 1 - c, z))

    def place(self):
        page, z = lax.axis_index("page"), lax.axis_index("band")
        return page // (2 * self.side), (page // 2) % self.side, page % 2, z


def after(value, *others):
    return lax.optimization_barrier((value, others))[0]


def z_direct(grid, shard):
    return [shard] + [grid.along_z(shard, step) for step in range(1, grid.bands)]


def z_ring(grid, shard):
    pieces = [shard]
    for _ in range(1, grid.bands):
        pieces.append(grid.along_z(pieces[-1], 1))
    return pieces


class Gather:
    def __init__(self, grid, pieces):
        self.grid = grid
        rows, width = pieces[0].shape
        z = lax.axis_index("band")
        block = jnp.zeros((grid.bands, rows, width), pieces[0].dtype)
        for step, piece in enumerate(pieces):
            block = lax.dynamic_update_slice(block, piece[None], ((z - step) % grid.bands, 0, 0))
        self.block = block.reshape(grid.bands * rows, width)

    def near_step(self, *pins):
        block = after(self.block, *pins)
        got = [self.grid.near(block, step) for step in range(1, self.grid.side)]
        self.near_all = jnp.stack([self.block] + got)

    def far_step(self, *pins):
        near_all = after(self.near_all, *pins)
        self.far_all = [self.grid.far(near_all, step) for step in range(1, self.grid.side)]

    def core_step(self, *pins):
        parts = [self.near_all] + self.far_all
        first = self.grid.across(after(self.near_all, *pins))
        return parts + [first] + [self.grid.across(item) for item in self.far_all]


def part_copies(grid, parts, whole, sems):
    i, j, c, _ = grid.place()
    tall = parts[0].shape[1]
    copies = []
    for d in range(2):
        core = (c + d) % 2
        for a in range(grid.side):
            for b in range(grid.side):
                di = jnp.where(core == 0, a, b)
                dj = jnp.where(core == 0, b, a)
                up = (i - di + grid.side) % grid.side
                left = (j - dj + grid.side) % grid.side
                index = (up * grid.side + left) * 2 + core
                copies.append(
                    pltpu.make_async_copy(
                        parts[d * grid.side + a].at[b],
                        whole.at[pl.ds(pl.multiple_of(index * tall, 8), tall), :],
                        sems.at[len(copies)],
                    )
                )
    return copies


def store_blocks(grid, source, first, cols, keep, send):
    i, j, c, _ = grid.place()
    tall = keep.shape[1]
    for n in range(source.shape[0] // tall):
        block = first + n
        core = block % 2
        ti, tj = block // (2 * grid.side), (block // 2) % grid.side
        di = (ti - i + grid.side) % grid.side
        dj = (tj - j + grid.side) % grid.side
        slot = di * grid.side + dj if core == 0 else dj * grid.side + di
        rows = slice(n * tall, (n + 1) * tall)

        @pl.when(c == core)
        def _():
            keep[slot, :, cols] = source[rows, :].astype(BF16)

        @pl.when(c != core)
        def _():
            send[slot, :, cols] = source[rows, :].astype(BF16)


class Sum:
    def __init__(self, grid, keep, send):
        self.grid, self.send = grid, send
        self.terms = [keep]

    def total(self, at):
        result = self.terms[0][at].astype(F32)
        for item in self.terms[1:]:
            result = result + item[at].astype(F32)
        return result

    def core_step(self, *pins):
        side = self.grid.side
        got = self.grid.across(self.send)
        self.terms = after(self.terms, *pins) + [got]
        self.send = [self.total(slice(a * side, (a + 1) * side)).astype(BF16) for a in range(1, side)]

    def far_step(self, *pins):
        side = self.grid.side
        got = [self.grid.far(item, a) for a, item in enumerate(self.send, 1)]
        self.terms = after(self.terms, *pins) + got
        self.send = [self.total(b).astype(BF16) for b in range(1, side)]

    def near_step(self, *pins):
        grid = self.grid
        got = [grid.near(item, b)[None] for b, item in enumerate(self.send, 1)]
        self.terms = after(self.terms, *pins) + got
        own = self.total(0)
        own = own.reshape(grid.bands, own.shape[0] // grid.bands, own.shape[1])
        z = lax.axis_index("band")
        self.own = lax.dynamic_index_in_dim(own, z, 0, False)
        self.send = [
            lax.dynamic_index_in_dim(own, (z + step) % grid.bands, 0, False).astype(BF16)
            for step in range(1, grid.bands)
        ]

    def z_step(self):
        for step, item in enumerate(self.send, 1):
            self.own = self.own + self.grid.along_z(item, step).astype(F32)
        return self.own


def pack_kernel(lengths, permutation, *refs):
    vectors, bias = refs[:8], refs[8]
    wq, wk, wv, wo, wi, wc = refs[9:15]
    a_out, b_out, c_out, doc_out = refs[15:19]
    stage, tall = refs[19:]
    rows, width = wq.shape
    docs = lengths.shape[1]
    tokens = permutation.shape[1]
    earlier = lax.broadcasted_iota(jnp.int32, (docs, docs), 1) <= lax.broadcasted_iota(
        jnp.int32, (docs, docs), 0
    )
    ends = jnp.sum(jnp.where(earlier, lengths[...], 0).astype(F32), axis=1, keepdims=True)
    marks = jnp.sum(
        jnp.where(permutation[...].astype(F32) >= ends, 1.0, 0.0), axis=0, keepdims=True
    )
    doc_out[...] = marks
    for n, item in enumerate((wq, None, None)):
        if item is not None:
            a_out[:, n * width : (n + 1) * width] = item[...].astype(BF16)
    for pair in range(width // PAIR):
        at = width + 2 * pair * PAIR
        cols = slice(pair * PAIR, (pair + 1) * PAIR)
        a_out[:, at : at + PAIR] = wk[:, cols].astype(BF16)
        a_out[:, at + PAIR : at + 2 * PAIR] = wv[:, cols].astype(BF16)
    stage[...] = jnp.zeros_like(stage)
    for n, item in enumerate(vectors):
        stage[n : n + 1, 0:rows] = item[...].reshape(1, rows)
    tall[...] = jnp.transpose(stage[...])
    tall[0:1, 16 : 16 + bias.shape[0]] = bias[...].reshape(1, bias.shape[0])
    a_out[:, 3 * width : 3 * width + 128] = tall[0:rows, :].astype(BF16)
    tall[...] = jnp.zeros_like(tall)
    for n in range(3):
        count = min(128, tokens - n * 128)
        tall[n : n + 1, 0:count] = marks[:, n * 128 : n * 128 + count]
    a_out[:, 3 * width + 128 :] = tall[0:rows, :].astype(BF16)
    b_out[:, :width] = wo[...].astype(BF16)
    b_out[:, width:] = wi[...].astype(BF16)
    c_out[...] = wc[...].astype(BF16)


def pack(lengths, permutation, vectors, bias, weights):
    rows, width = weights[0].shape
    wide = weights[4].shape[1]
    tokens = permutation.shape[1]
    assert tokens <= 3 * 128 and bias.shape[0] <= 112 and rows <= 128
    vmem = pl.BlockSpec(memory_space=pltpu.VMEM)
    return pl.pallas_call(
        pack_kernel,
        in_specs=[vmem] * 17,
        out_specs=[vmem] * 4,
        out_shape=[
            jax.ShapeDtypeStruct((rows, 3 * width + SLAB), BF16),
            jax.ShapeDtypeStruct((rows, width + wide), BF16),
            jax.ShapeDtypeStruct(weights[5].shape, BF16),
            jax.ShapeDtypeStruct((1, tokens), F32),
        ],
        scratch_shapes=[pltpu.VMEM((128, 128), F32), pltpu.VMEM((128, 128), F32)],
        compiler_params=pltpu.CompilerParams(vmem_limit_bytes=VMEM_LIMIT),
        cost_estimate=CHEAP,
        name="pack",
    )(lengths, permutation, *vectors, bias, *weights)


def head_mask(rows, head):
    lanes = lax.broadcasted_iota(jnp.int32, (rows, PAIR), 1)
    return (lanes // HEAD_DIM) == head


def attend_kernel(grid, pieces, parts, *refs):
    hidden, refs = refs[:pieces], refs[pieces:]
    part_refs, refs = refs[:parts], refs[parts:]
    own_doc, all_doc = refs[:2]
    q_out, kv_out, att_out, log_out, vec_out, bias_out, bias, weights, slab, sems = refs[2:]
    tokens = q_out.shape[0]
    keys = kv_out.shape[0]
    width = weights.shape[0]
    step = q_out.shape[1]
    group = pl.program_id(0)

    @pl.when(group == 0)
    def _():
        copies = part_copies(grid, part_refs, weights, sems)
        for copy in copies:
            copy.start()
        bias[...] = jnp.where(own_doc[...] == all_doc[...], 0.0, -1e30).astype(F32)
        for copy in copies:
            copy.wait()
        slab[...] = weights[:, 3 * width : 3 * width + 128].astype(F32)
        vec_out[...] = jnp.transpose(slab[...])[0:16, :]
        rows = width // grid.devices
        count = bias_out.shape[1] // grid.devices
        for n in range(grid.devices):
            bias_out[:, n * count : (n + 1) * count] = slab[n * rows : n * rows + 1, 16 : 16 + count]

    at = pl.multiple_of(group * step, step)
    query_bias = vec_out[0:1, pl.ds(at, step)]
    value_bias = vec_out[1:2, pl.ds(at, step)]
    q_out[...] = (dot(hidden[0][...], weights[:, pl.ds(at, step)]) + query_bias).astype(BF16)
    pairs = step // PAIR
    for p in range(pieces):
        rows = slice(p * tokens, (p + 1) * tokens)
        for pair in range(pairs):
            there = pl.multiple_of(width + 2 * at + 2 * pair * PAIR, 2 * PAIR)
            both = dot(hidden[p][...], weights[:, pl.ds(there, 2 * PAIR)])
            to = 2 * pair * PAIR
            kv_out[rows, to : to + PAIR] = both[:, :PAIR].astype(BF16)
            value = both[:, PAIR:] + value_bias[:, pair * PAIR : (pair + 1) * PAIR]
            kv_out[rows, to + PAIR : to + 2 * PAIR] = value.astype(BF16)
    lane = lax.broadcasted_iota(jnp.int32, (tokens, 128), 1)
    logs = jnp.zeros((tokens, 128), F32)
    ones = jnp.ones((keys, PAIR), BF16)
    for pair in range(pairs):
        cols = slice(pair * PAIR, (pair + 1) * PAIR)
        query = q_out[:, cols]
        key = kv_out[:, 2 * pair * PAIR : (2 * pair + 1) * PAIR]
        value = jnp.concatenate([kv_out[:, (2 * pair + 1) * PAIR : (2 * pair + 2) * PAIR], ones], axis=1)
        outs = []
        for head in range(2):
            picked = jnp.where(head_mask(tokens, head), query * HEAD_DIM**-0.5, 0).astype(BF16)
            scores = times_transposed(picked, key) + bias[...]
            peak = jnp.max(scores, axis=1, keepdims=True)
            weights = jnp.exp(scores - peak).astype(BF16)
            both = dot(weights, value)
            outs.append(both[:, :PAIR] / both[:, PAIR:])
            total = peak + jnp.log(both[:, PAIR:])
            logs = jnp.where(lane == pair * 2 + head, total, logs)
        att_out[:, cols] = jnp.where(head_mask(tokens, 0), outs[0], outs[1]).astype(BF16)
    log_out[...] = logs[None]


ANY = pl.BlockSpec(memory_space=pl.ANY)
VMEM = pl.BlockSpec(memory_space=pltpu.VMEM)


def attend(grid, hidden, parts, own_doc, all_doc, wide):
    pieces = len(hidden)
    tokens, width = hidden[0].shape
    keys = pieces * tokens
    step = 256
    groups = width // step
    whole = lambda shape: pl.BlockSpec(shape, lambda g: (0, 0))
    tall = lambda rows: pl.BlockSpec((rows, step), lambda g: (0, g))
    return pl.pallas_call(
        functools.partial(attend_kernel, grid, pieces, len(parts)),
        grid=(groups,),
        in_specs=[whole(item.shape) for item in hidden]
        + [ANY] * len(parts)
        + [whole(own_doc.shape), whole(all_doc.shape)],
        out_specs=[
            tall(tokens),
            pl.BlockSpec((keys, 2 * step), lambda g: (0, g)),
            tall(tokens),
            pl.BlockSpec((1, tokens, 128), lambda g: (g, 0, 0)),
            whole((16, width)),
            whole((1, wide)),
        ],
        out_shape=[
            jax.ShapeDtypeStruct((tokens, width), BF16),
            jax.ShapeDtypeStruct((keys, 2 * width), BF16),
            jax.ShapeDtypeStruct((tokens, width), BF16),
            jax.ShapeDtypeStruct((groups, tokens, 128), F32),
            jax.ShapeDtypeStruct((16, width), F32),
            jax.ShapeDtypeStruct((1, wide), F32),
        ],
        scratch_shapes=[
            pltpu.VMEM((tokens, keys), F32),
            pltpu.VMEM((width, parts[0].shape[2]), BF16),
            pltpu.VMEM((width, 128), F32),
            pltpu.SemaphoreType.DMA((2 * grid.quads,)),
        ],
        compiler_params=pltpu.CompilerParams(vmem_limit_bytes=VMEM_LIMIT),
        cost_estimate=CHEAP,
        name="attend",
    )(*hidden, *parts, own_doc, all_doc)


def attend_back_kernel(start, q, kv, grad, att, logs, own_doc, doc, dq_out, dkv_out, sum_out, bias):
    tokens = q.shape[0]
    pair = pl.program_id(0) + start

    @pl.when(pair == start)
    def _():
        bias[...] = jnp.where(own_doc[...] == doc[...], 0.0, -1e30).astype(F32)

    lane = lax.broadcasted_iota(jnp.int32, (tokens, 128), 1)
    key, value = kv[:, :PAIR], kv[:, PAIR:]
    product = grad[...].astype(F32) * att[...].astype(F32)
    dq, dk, dv = [], 0.0, 0.0
    for head in range(2):
        mask = head_mask(tokens, head)
        query = jnp.where(mask, q[...] * HEAD_DIM**-0.5, 0).astype(BF16)
        part = jnp.where(mask, grad[...], 0).astype(BF16)
        slot = (pair % 2) * 2 + head
        log_total = jnp.sum(jnp.where(lane == slot, logs[0], 0.0), axis=1, keepdims=True)
        inner = jnp.sum(jnp.where(mask, product, 0.0), axis=1, keepdims=True)
        weights = jnp.exp(times_transposed(query, key) + bias[...] - log_total)
        back = (weights * (times_transposed(part, value) - inner)).astype(BF16)
        dq.append(dot(back, key) * HEAD_DIM**-0.5)
        dk = dk + outer_sum(back, query)
        dv = dv + outer_sum(weights.astype(BF16), part)
    dq_low = jnp.where(head_mask(tokens, 0), dq[0], dq[1]).astype(BF16)
    dq_out[...] = dq_low
    dkv_out[:, :PAIR] = dk.astype(BF16)
    dv_low = dv.astype(BF16)
    dkv_out[:, PAIR:] = dv_low
    sum_out[0:1, :] = column_sum(dq_low)
    sum_out[1:2, :] = column_sum(dv_low)


def attend_back(start, pairs, q, kv, grad, att, logs, own_doc, all_doc):
    tokens = q.shape[0]
    keys = kv.shape[0]
    short = pl.BlockSpec((tokens, PAIR), lambda g: (0, start + g))
    whole = lambda shape: pl.BlockSpec(shape, lambda g: (0, 0))
    return pl.pallas_call(
        functools.partial(attend_back_kernel, start),
        grid=(pairs,),
        in_specs=[
            short,
            pl.BlockSpec((keys, 2 * PAIR), lambda g: (0, start + g)),
            short,
            short,
            pl.BlockSpec((1, tokens, 128), lambda g: ((start + g) // 2, 0, 0)),
            whole(own_doc.shape),
            whole(all_doc.shape),
        ],
        out_specs=[
            pl.BlockSpec((tokens, PAIR), lambda g: (0, g)),
            pl.BlockSpec((keys, 2 * PAIR), lambda g: (0, g)),
            pl.BlockSpec((8, PAIR), lambda g: (0, g)),
        ],
        out_shape=[
            jax.ShapeDtypeStruct((tokens, pairs * PAIR), BF16),
            jax.ShapeDtypeStruct((keys, 2 * pairs * PAIR), BF16),
            jax.ShapeDtypeStruct((8, pairs * PAIR), F32),
        ],
        scratch_shapes=[pltpu.VMEM((tokens, keys), F32)],
        compiler_params=pltpu.CompilerParams(vmem_limit_bytes=VMEM_LIMIT),
        cost_estimate=CHEAP,
        name="attend_back",
    )(q, kv, grad, att, logs, own_doc, all_doc)


def interleave(key, value):
    rows, width = key.shape
    split = lambda item: item.reshape(rows, width // PAIR, 1, PAIR)
    return jnp.concatenate([split(key), split(value)], axis=2).reshape(rows, 2 * width)


def part_of(both, which):
    rows, width = both.shape
    return both.reshape(rows, width // (2 * PAIR), 2, PAIR)[:, :, which].reshape(rows, width // 2)


def row_mean(values):
    return jnp.mean(values, axis=-1, keepdims=True)


def column_sum(values):
    return jnp.sum(values.astype(F32), axis=0, keepdims=True)


def norm_back(grad_out, normed, inverse, scale_gain):
    grad_normed = grad_out * scale_gain
    inner = grad_normed - row_mean(grad_normed) - normed * row_mean(grad_normed * normed)
    return inner * inverse


def normalize(values):
    centred = values - row_mean(values)
    inverse = lax.rsqrt(row_mean(centred * centred) + EPSILON)
    return centred * inverse, inverse


def middle_kernel(grid, parts, att, hidden, cotangent, vec, b_expand, *refs):
    parts_b, parts_c, refs = refs[:parts], refs[parts : 2 * parts], refs[2 * parts :]
    result, first_out, normed_out, inverse_out, slope, second_out, low_out, keep, send, sums = refs[:10]
    wb, wc, active, total, sem_b, sem_c = refs[10:]
    width, wide = wb.shape[0], wc.shape[0]
    copies_b = part_copies(grid, parts_b, wb, sem_b)
    copies_c = part_copies(grid, parts_c, wc, sem_c)
    for copy in copies_b + copies_c:
        copy.start()
    for copy in copies_b:
        copy.wait()
    mixed = dot(att[...], wb[:, :width]) + vec[2:3, :]
    normed, inverse = normalize(hidden[...].astype(F32) + mixed)
    normed_out[...] = normed
    inverse_out[...] = jnp.broadcast_to(inverse, inverse_out.shape)
    first = normed * vec[3:4, :] + vec[4:5, :]
    first_out[...] = first.astype(BF16)
    for n in range(wide // width):
        cols = slice(n * width, (n + 1) * width)
        into = dot(first_out[...], wb[:, width + n * width : width + (n + 1) * width]) + b_expand[:, cols]
        chance = 0.5 * (1.0 + lax.erf(into * (0.5**0.5)))
        density = jnp.exp(-0.5 * into * into) * ((2.0 * math.pi) ** -0.5)
        active[:, cols] = (into * chance).astype(BF16)
        slope[:, cols] = (chance + into * density).astype(BF16)
    for copy in copies_c:
        copy.wait()
    contracted = dot(active[...], wc[...]) + vec[5:6, :]
    normed, inverse = normalize(first + contracted)
    result[...] = (normed * vec[6:7, :] + vec[7:8, :]).astype(BF16)
    grad = cotangent[...].astype(F32)
    second = norm_back(grad, normed, inverse, vec[6:7, :])
    second_out[...] = second
    low = second.astype(BF16)
    low_out[...] = low
    sums[...] = jnp.zeros_like(sums)
    sums[5:6, :] = column_sum(low)
    sums[6:7, :] = column_sum(grad * normed)
    sums[7:8, :] = column_sum(grad)
    blocks = width // keep.shape[1]
    for n in range(wide // width):
        total[...] = outer_sum(active[:, n * width : (n + 1) * width], low)
        store_blocks(grid, total, n * blocks, slice(0, width), keep, send)


def middle(grid, att, hidden, cotangent, vec, b_expand, parts_b, parts_c):
    tokens, width = hidden.shape
    wide = b_expand.shape[1]
    blocks = jax.ShapeDtypeStruct((grid.quads,) + parts_c[0].shape[1:], BF16)
    return pl.pallas_call(
        functools.partial(middle_kernel, grid, len(parts_b)),
        in_specs=[VMEM] * 5 + [ANY] * (2 * len(parts_b)),
        out_specs=[VMEM] * 10,
        out_shape=[
            jax.ShapeDtypeStruct((tokens, width), BF16),
            jax.ShapeDtypeStruct((tokens, width), BF16),
            jax.ShapeDtypeStruct((tokens, width), F32),
            jax.ShapeDtypeStruct((tokens, 128), F32),
            jax.ShapeDtypeStruct((tokens, wide), BF16),
            jax.ShapeDtypeStruct((tokens, width), F32),
            jax.ShapeDtypeStruct((tokens, width), BF16),
            blocks,
            blocks,
            jax.ShapeDtypeStruct((8, width), F32),
        ],
        scratch_shapes=[
            pltpu.VMEM((width, width + wide), BF16),
            pltpu.VMEM((wide, width), BF16),
            pltpu.VMEM((tokens, wide), BF16),
            pltpu.VMEM((width, width), F32),
            pltpu.SemaphoreType.DMA((2 * grid.quads,)),
            pltpu.SemaphoreType.DMA((2 * grid.quads,)),
        ],
        compiler_params=pltpu.CompilerParams(vmem_limit_bytes=VMEM_LIMIT),
        cost_estimate=CHEAP,
        name="middle",
    )(att, hidden, cotangent, vec, b_expand, *parts_b, *parts_c)


def dense_back_kernel(grid, parts, att, first, normed, inverse, slope, second, low, vec, *refs):
    parts_b, parts_c, refs = refs[:parts], refs[parts : 2 * parts], refs[2 * parts :]
    grad_sum, att_back, keep, send, sums, bias_sum = refs[:6]
    wb, wc, back, total, sem_b, sem_c = refs[6:]
    width, wide = wb.shape[0], wc.shape[0]
    copies_b = part_copies(grid, parts_b, wb, sem_b)
    copies_c = part_copies(grid, parts_c, wc, sem_c)
    for copy in copies_c + copies_b:
        copy.start()
    for copy in copies_c:
        copy.wait()
    for n in range(wide // width):
        cols = slice(n * width, (n + 1) * width)
        piece = (times_transposed(low[...], wc[cols, :]) * slope[:, cols].astype(F32)).astype(BF16)
        back[:, cols] = piece
        bias_sum[:, cols] = column_sum(piece)
    for copy in copies_b:
        copy.wait()
    grad_first = second[...] + times_transposed(back[...], wb[:, width:])
    grad = norm_back(grad_first, normed[...], inverse[:, 0:1], vec[3:4, :])
    grad_sum[...] = grad
    mixed = grad.astype(BF16)
    att_back[...] = times_transposed(mixed, wb[:, :width]).astype(BF16)
    sums[...] = jnp.zeros_like(sums)
    sums[2:3, :] = column_sum(mixed)
    sums[3:4, :] = column_sum(grad_first * normed[...])
    sums[4:5, :] = column_sum(grad_first)
    total[...] = outer_sum(att[...], mixed)
    store_blocks(grid, total, 0, slice(0, width), keep, send)
    for n in range(wide // width):
        total[...] = outer_sum(first[...], back[:, n * width : (n + 1) * width])
        store_blocks(grid, total, 0, slice((n + 1) * width, (n + 2) * width), keep, send)


def dense_back(grid, att, first, normed, inverse, slope, second, low, vec, parts_b, parts_c):
    tokens, width = att.shape
    wide = slope.shape[1]
    blocks = jax.ShapeDtypeStruct((grid.quads,) + parts_b[0].shape[1:], BF16)
    return pl.pallas_call(
        functools.partial(dense_back_kernel, grid, len(parts_b)),
        in_specs=[VMEM] * 8 + [ANY] * (2 * len(parts_b)),
        out_specs=[VMEM] * 6,
        out_shape=[
            jax.ShapeDtypeStruct((tokens, width), F32),
            jax.ShapeDtypeStruct((tokens, width), BF16),
            blocks,
            blocks,
            jax.ShapeDtypeStruct((8, width), F32),
            jax.ShapeDtypeStruct((1, wide), F32),
        ],
        scratch_shapes=[
            pltpu.VMEM((width, width + wide), BF16),
            pltpu.VMEM((wide, width), BF16),
            pltpu.VMEM((tokens, wide), BF16),
            pltpu.VMEM((width, width), F32),
            pltpu.SemaphoreType.DMA((2 * grid.quads,)),
            pltpu.SemaphoreType.DMA((2 * grid.quads,)),
        ],
        compiler_params=pltpu.CompilerParams(vmem_limit_bytes=VMEM_LIMIT),
        cost_estimate=CHEAP,
        name="dense_back",
    )(att, first, normed, inverse, slope, second, low, vec, *parts_b, *parts_c)


def input_back_kernel(grid, parts, grad_sum, dq0, dq1, dkv0, dkv1, *refs):
    part_refs, outs = refs[:parts], refs[parts:-2]
    weights, sems = refs[-2:]
    tokens = grad_sum.shape[0]
    width = weights.shape[0]
    half = dkv0.shape[1]
    copies = part_copies(grid, part_refs, weights, sems)
    for copy in copies:
        copy.start()
    for copy in copies:
        copy.wait()
    for piece in range(len(outs) - 1, -1, -1):
        rows = slice(piece * tokens, (piece + 1) * tokens)
        back = times_transposed(dkv0[rows, :], weights[:, width : width + half])
        back = back + times_transposed(dkv1[rows, :], weights[:, width + half : 3 * width])
        if piece == 0:
            back = back + times_transposed(dq0[...], weights[:, : half // 2])
            back = back + times_transposed(dq1[...], weights[:, half // 2 : width])
            back = back + grad_sum[...]
        outs[piece][...] = back.astype(outs[piece].dtype)


def input_back(grid, grad_sum, first_part, last_part, parts):
    tokens, width = grad_sum.shape
    return pl.pallas_call(
        functools.partial(input_back_kernel, grid, len(parts)),
        in_specs=[VMEM] * 5 + [ANY] * len(parts),
        out_specs=[VMEM] * grid.bands,
        out_shape=[jax.ShapeDtypeStruct((tokens, width), F32)]
        + [jax.ShapeDtypeStruct((tokens, width), BF16)] * (grid.bands - 1),
        scratch_shapes=[
            pltpu.VMEM((width, parts[0].shape[2]), BF16),
            pltpu.SemaphoreType.DMA((2 * grid.quads,)),
        ],
        compiler_params=pltpu.CompilerParams(vmem_limit_bytes=VMEM_LIMIT),
        cost_estimate=CHEAP,
        name="input_back",
    )(grad_sum, first_part[0], last_part[0], first_part[1], last_part[1], *parts)


def weight_back_kernel(grid, pieces, *refs):
    hidden, refs = refs[:pieces], refs[pieces:]
    dq0, dq1, dkv0, dkv1, sum0, sum1, sum2, sum3, bias_sum, keep, send, every, total, stage, slab = refs
    tokens, width = hidden[0].shape
    half = dkv0.shape[1]
    for n in range(pieces):
        every[n * tokens : (n + 1) * tokens, :] = hidden[n][...]
    for n, item in enumerate((dkv0, dkv1)):
        total[:, 0:half] = outer_sum(every[...], item[...])
        store_blocks(grid, total, 0, slice(width + n * half, width + (n + 1) * half), keep, send)
    for n, item in enumerate((dq0, dq1)):
        total[:, n * half // 2 : (n + 1) * half // 2] = outer_sum(hidden[0][...], item[...])
    store_blocks(grid, total, 0, slice(0, width), keep, send)
    stage[...] = jnp.zeros_like(stage)
    stage[0:8, :] = sum2[...] + sum3[...]
    for n, item in enumerate((sum0, sum1)):
        stage[0:2, n * half // 2 : (n + 1) * half // 2] = item[0:2, :]
    slab[:, :128] = jnp.transpose(stage[...])
    slab[:, 128:] = jnp.zeros((width, SLAB - 128), F32)
    rows = width // grid.devices
    count = bias_sum.shape[1] // grid.devices
    for n in range(grid.devices):
        slab[n * rows : n * rows + 1, 16 : 16 + count] = bias_sum[:, n * count : (n + 1) * count]
    store_blocks(grid, slab, 0, slice(3 * width, 3 * width + SLAB), keep, send)


def weight_back(grid, hidden, first_part, last_part, sums, bias_sum):
    pieces = len(hidden)
    tokens, width = hidden[0].shape
    tall = width // (2 * grid.quads)
    blocks = jax.ShapeDtypeStruct((grid.quads, tall, 3 * width + SLAB), BF16)
    return pl.pallas_call(
        functools.partial(weight_back_kernel, grid, pieces),
        in_specs=[VMEM] * (pieces + 9),
        out_specs=[VMEM] * 2,
        out_shape=[blocks, blocks],
        scratch_shapes=[
            pltpu.VMEM((pieces * tokens, width), BF16),
            pltpu.VMEM((width, width), F32),
            pltpu.VMEM((128, width), F32),
            pltpu.VMEM((width, SLAB), F32),
        ],
        compiler_params=pltpu.CompilerParams(vmem_limit_bytes=VMEM_LIMIT),
        cost_estimate=CHEAP,
        name="weight_back",
    )(
        *hidden,
        first_part[0],
        last_part[0],
        first_part[1],
        last_part[1],
        first_part[2],
        last_part[2],
        *sums,
        bias_sum,
    )


def per_device(
    grid,
    hidden_in,
    lengths,
    permutation,
    query_weight,
    query_bias,
    key_weight,
    value_weight,
    value_bias,
    mix_weight,
    mix_bias,
    first_gain,
    first_shift,
    expand_weight,
    expand_bias,
    contract_weight,
    contract_bias,
    second_gain,
    second_shift,
    cotangent,
):
    tokens, width = hidden_in.shape
    wide = contract_weight.shape[0] * grid.devices
    rows = query_weight.shape[0]
    bands = grid.bands

    vectors = [query_bias, value_bias, mix_bias, first_gain, first_shift, contract_bias, second_gain, second_shift]
    weights = [query_weight, key_weight, value_weight, mix_weight, expand_weight, contract_weight]
    shard_a, shard_b, shard_c, doc = pack(lengths, permutation, vectors, expand_bias, weights)

    messages = [hidden_in, grid.along_z(hidden_in, 1)]
    pieces_a = z_direct(grid, shard_a)
    pieces_b = z_direct(grid, after(shard_b, *pieces_a))
    gather_a = Gather(grid, pieces_a)
    gather_a.near_step()
    messages.append(grid.along_z(after(messages[-1], *pieces_a), 1))
    pieces_c = z_direct(grid, after(shard_c, *pieces_b, gather_a.near_all))
    gather_b, gather_c = Gather(grid, pieces_b), Gather(grid, pieces_c)
    gather_a.far_step()
    gather_b.near_step()
    for step in range(3, bands):
        messages.append(grid.along_z(after(messages[-1], *pieces_b), 1))
    gather_c.near_step(*gather_a.far_all)
    gather_b.far_step(*gather_a.far_all)
    parts_a = gather_a.core_step()
    gather_c.far_step()
    messages[0] = after(messages[0], gather_c.near_all, gather_b.near_all)
    parts_b = gather_b.core_step()

    docs_of = [doc] + [
        item[0:3, 3 * width + 128 :].astype(F32).reshape(1, 3 * 128)[:, :tokens] for item in pieces_a[1:]
    ]
    all_doc = jnp.concatenate(docs_of, axis=1)
    own_doc = doc.reshape(tokens, 1)
    q, kv, attended, logs, vec, b_expand = attend(grid, messages, parts_a, own_doc, all_doc, wide)
    gather_c.far_all = after(gather_c.far_all, attended)
    parts_c = gather_c.core_step()
    result, first, normed, inverse, slope, second, low, keep, send, sums_two = middle(
        grid, attended, hidden_in, cotangent, vec, b_expand, parts_b, parts_c
    )
    sum_c = Sum(grid, keep, send)
    sum_c.core_step()
    low = after(low, *sum_c.send)
    grad_sum, attended_back, keep, send, sums_one, d_b_expand = dense_back(
        grid, attended, first, normed, inverse, slope, second, low, vec, parts_b, parts_c
    )
    sum_b = Sum(grid, keep, send)
    sum_c.far_step(grad_sum)
    attended_back = after(attended_back, sum_c.send)

    pairs = width // PAIR
    half = pairs // 2
    first_part = attend_back(0, half, q, kv, attended_back, attended, logs, own_doc, all_doc)
    sum_c.near_step(first_part)
    sum_b.core_step(sum_c.send)
    attended_back = after(attended_back, sum_b.send, sum_c.send)
    last_part = attend_back(half, pairs - half, q, kv, attended_back, attended, logs, own_doc, all_doc)
    backs = input_back(grid, grad_sum, first_part, last_part, parts_a)
    sum_b.far_step(backs)
    last_part = after(last_part, backs, sum_b.send)
    keep, send = weight_back(grid, messages, first_part, last_part, (sums_two, sums_one), d_b_expand)
    sum_a = Sum(grid, keep, send)
    sent = backs[bands - 1]
    for piece in range(bands - 1, 0, -1):
        got = grid.along_z(sent, -1)
        pins = (keep,) if piece == bands - 1 else tuple(sum_b.send)
        sent = after(backs[piece - 1], *pins).astype(F32) + got.astype(F32)
        if piece > 1:
            sent = sent.astype(BF16)
        if piece == bands - 1:
            sum_a.core_step(sent)
            sum_b.near_step(sum_a.send)
        elif piece == bands - 2:
            sum_a.far_step(sent)
    grad_input = sent
    sum_a.near_step()
    d_contract = sum_c.z_step()
    d_b = sum_b.z_step()
    d_a = sum_a.z_step()
    slab = d_a[:, 3 * width :]
    small = [slab[:, n] for n in range(8)]
    d_both = d_a[:, width : 3 * width]
    return (
        result,
        grad_input.astype(BF16),
        d_a[:, :width],
        small[0],
        part_of(d_both, 0),
        part_of(d_both, 1),
        small[1],
        d_b[:, :width],
        small[2],
        small[3],
        small[4],
        d_b[:, width:],
        slab[0, 16 : 16 + expand_bias.shape[0]],
        d_contract,
        small[5],
        small[6],
        small[7],
    )


def solution(mesh):
    grid = Grid(mesh.shape["page"], mesh.shape["band"])
    matrix, vector = P(AXES, None), P(AXES)
    parameters = (
        matrix,
        vector,
        matrix,
        matrix,
        vector,
        matrix,
        vector,
        vector,
        vector,
        matrix,
        vector,
        matrix,
        vector,
        vector,
        vector,
    )
    return jax.shard_map(
        functools.partial(per_device, grid),
        mesh=mesh,
        in_specs=(matrix, P("page", None), P("page", "band")) + parameters + (matrix,),
        out_specs=(matrix, matrix) + parameters,
        check_vma=False,
    )
```

```python
import functools
import itertools
import math

import jax
import jax.numpy as jnp
from jax import lax
from jax.experimental import pallas as pl
from jax.experimental.pallas import tpu as pltpu
from jax.sharding import PartitionSpec as P

HEAD_DIM = 64
PAIR = 2 * HEAD_DIM
EPSILON = 1e-12
AXES = ("page", "band")
SLAB = 256
BF16, F32 = jnp.bfloat16, jnp.float32
LIMITS = {
    "pack": 60,
    "attend": 44,
    "middle": 36,
    "dense_back": 36,
    "attend_back": 50,
    "input_back": 32,
    "weight_back": 32,
}


def limit(kernel):
    return pltpu.CompilerParams(vmem_limit_bytes=LIMITS[kernel] * 2**20)


def cost(microseconds):
    return pl.CostEstimate(flops=int(microseconds * 1.1e9), bytes_accessed=1024, transcendentals=0)


def dot(left, right):
    return lax.dot_general(left, right, (((1,), (0,)), ((), ())), preferred_element_type=F32)


def times_transposed(left, right):
    return lax.dot_general(left, right, (((1,), (1,)), ((), ())), preferred_element_type=F32)


def outer_sum(left, right):
    return lax.dot_general(left, right, (((0,), (0,)), ((), ())), preferred_element_type=F32)


class Grid:
    def __init__(self, pages, bands):
        self.side = math.isqrt(pages // 2)
        assert self.side * self.side * 2 == pages
        self.bands = bands
        self.devices = pages * bands
        self.quads = self.side * self.side

    def linear(self, i, j, c, z):
        return ((i * self.side + j) * 2 + c) * self.bands + z

    def permute(self, array, move):
        side, bands = self.side, self.bands
        pairs = []
        for i, j, c, z in itertools.product(range(side), range(side), range(2), range(bands)):
            ti, tj, tc, tz = move(i, j, c, z)
            pairs.append((self.linear(i, j, c, z), self.linear(ti % side, tj % side, tc, tz % bands)))
        return lax.ppermute(array, AXES, pairs)

    def along_z(self, array, step):
        return self.permute(array, lambda i, j, c, z: (i, j, c, z + step))

    def near(self, array, step):
        return self.permute(
            array, lambda i, j, c, z: (i, j + step, c, z) if c == 0 else (i + step, j, c, z)
        )

    def far(self, array, step):
        return self.permute(
            array, lambda i, j, c, z: (i + step, j, c, z) if c == 0 else (i, j + step, c, z)
        )

    def across(self, array):
        return self.permute(array, lambda i, j, c, z: (i, j, 1 - c, z))

    def place(self):
        page, z = lax.axis_index("page"), lax.axis_index("band")
        return page // (2 * self.side), (page // 2) % self.side, page % 2, z


def after(value, *others):
    return lax.optimization_barrier((value, others))[0]


def z_direct(grid, shard):
    return [shard] + [grid.along_z(shard, step) for step in range(1, grid.bands)]


def z_ring(grid, shard):
    pieces = [shard]
    for _ in range(1, grid.bands):
        pieces.append(grid.along_z(pieces[-1], 1))
    return pieces


class Gather:
    def __init__(self, grid, pieces):
        self.grid = grid
        rows, width = pieces[0].shape
        z = lax.axis_index("band")
        block = jnp.zeros((grid.bands, rows, width), pieces[0].dtype)
        for step, piece in enumerate(pieces):
            block = lax.dynamic_update_slice(block, piece[None], ((z - step) % grid.bands, 0, 0))
        self.block = block.reshape(grid.bands * rows, width)

    def near_step(self, *pins):
        block = after(self.block, *pins)
        got = [self.grid.near(block, step) for step in range(1, self.grid.side)]
        self.near_all = jnp.stack([self.block] + got)

    def far_step(self, *pins):
        near_all = after(self.near_all, *pins)
        self.far_all = [self.grid.far(near_all, step) for step in range(1, self.grid.side)]

    def core_step(self, *pins):
        parts = [self.near_all] + self.far_all
        first = self.grid.across(after(self.near_all, *pins))
        return parts + [first] + [self.grid.across(item) for item in self.far_all]


def fetch(grid, parts, whole, sems, cols):
    i, j, c, _ = grid.place()
    tall = parts[0].shape[1]
    for d in range(2):
        core = (c + d) % 2
        for a in range(grid.side):
            for b in range(grid.side):
                di = jnp.where(core == 0, a, b)
                dj = jnp.where(core == 0, b, a)
                up = (i - di + grid.side) % grid.side
                left = (j - dj + grid.side) % grid.side
                index = (up * grid.side + left) * 2 + core
                pltpu.make_async_copy(
                    parts[d * grid.side + a].at[b, :, cols],
                    whole.at[pl.ds(pl.multiple_of(index * tall, 8), tall), cols],
                    sems.at[index],
                ).start()


def fetched(parts, whole, sems, cols, blocks):
    tall = parts[0].shape[1]
    for n in blocks:
        pltpu.make_async_copy(
            parts[0].at[0, :, cols], whole.at[pl.ds(n * tall, tall), cols], sems.at[n]
        ).wait()


def store_blocks(grid, staged, first, blocks, cols, keep, send, sems):
    i, j, c, _ = grid.place()
    tall = keep.shape[1]
    for n in range(blocks):
        block = first + n
        core = block % 2
        ti, tj = block // (2 * grid.side), (block // 2) % grid.side
        di = (ti - i + grid.side) % grid.side
        dj = (tj - j + grid.side) % grid.side
        slot = di * grid.side + dj if core == 0 else dj * grid.side + di
        source = staged.at[pl.ds(block * tall, tall), cols]

        @pl.when(c == core)
        def _():
            pltpu.make_async_copy(source, keep.at[slot, :, cols], sems.at[block]).start()

        @pl.when(c != core)
        def _():
            pltpu.make_async_copy(source, send.at[slot, :, cols], sems.at[block]).start()


def stored(grid, staged, blocks, cols, keep, sems):
    tall = keep.shape[1]
    for block in blocks:
        source = staged.at[pl.ds(block * tall, tall), cols]
        pltpu.make_async_copy(source, keep.at[0, :, cols], sems.at[block]).wait()


class Sum:
    def __init__(self, grid, keep, send):
        self.grid, self.send = grid, send
        self.terms = [keep]

    def total(self, at):
        result = self.terms[0][at].astype(F32)
        for item in self.terms[1:]:
            result = result + item[at].astype(F32)
        return result

    def core_step(self, *pins):
        side = self.grid.side
        got = self.grid.across(self.send)
        self.terms = after(self.terms, *pins) + [got]
        self.send = [self.total(slice(a * side, (a + 1) * side)).astype(BF16) for a in range(1, side)]

    def far_step(self, *pins):
        side = self.grid.side
        got = [self.grid.far(item, a) for a, item in enumerate(self.send, 1)]
        self.terms = after(self.terms, *pins) + got
        self.send = [self.total(b).astype(BF16) for b in range(1, side)]

    def near_step(self, *pins):
        grid = self.grid
        got = [grid.near(item, b)[None] for b, item in enumerate(self.send, 1)]
        self.terms = after(self.terms, *pins) + got
        own = self.total(0)
        own = own.reshape(grid.bands, own.shape[0] // grid.bands, own.shape[1])
        z = lax.axis_index("band")
        self.own = lax.dynamic_index_in_dim(own, z, 0, False)
        self.send = [
            lax.dynamic_index_in_dim(own, (z + step) % grid.bands, 0, False).astype(BF16)
            for step in range(1, grid.bands)
        ]

    def z_step(self, *pins):
        self.own = after(self.own, *pins)
        for step, item in enumerate(self.send, 1):
            self.own = self.own + self.grid.along_z(item, step).astype(F32)
        return self.own


def pack_kernel(lengths, permutation, *refs):
    vectors, bias = refs[:8], refs[8]
    wq, wk, wv, wo, wi, wc = refs[9:15]
    a_out, b_out, c_out, doc_out = refs[15:19]
    stage, tall = refs[19:]
    rows, width = wq.shape
    docs = lengths.shape[1]
    tokens = permutation.shape[1]
    earlier = lax.broadcasted_iota(jnp.int32, (docs, docs), 1) <= lax.broadcasted_iota(
        jnp.int32, (docs, docs), 0
    )
    ends = jnp.sum(jnp.where(earlier, lengths[...], 0).astype(F32), axis=1, keepdims=True)
    marks = jnp.sum(
        jnp.where(permutation[...].astype(F32) >= ends, 1.0, 0.0), axis=0, keepdims=True
    )
    doc_out[...] = marks
    for n, item in enumerate((wq, None, None)):
        if item is not None:
            a_out[:, n * width : (n + 1) * width] = item[...].astype(BF16)
    for pair in range(width // PAIR):
        at = width + 2 * pair * PAIR
        cols = slice(pair * PAIR, (pair + 1) * PAIR)
        a_out[:, at : at + PAIR] = wk[:, cols].astype(BF16)
        a_out[:, at + PAIR : at + 2 * PAIR] = wv[:, cols].astype(BF16)
    stage[...] = jnp.zeros_like(stage)
    for n, item in enumerate(vectors):
        stage[n : n + 1, 0:rows] = item[...].reshape(1, rows)
    tall[...] = jnp.transpose(stage[...])
    tall[0:1, 16 : 16 + bias.shape[0]] = bias[...].reshape(1, bias.shape[0])
    a_out[:, 3 * width : 3 * width + 128] = tall[0:rows, :].astype(BF16)
    tall[...] = jnp.zeros_like(tall)
    for n in range(3):
        count = min(128, tokens - n * 128)
        tall[n : n + 1, 0:count] = marks[:, n * 128 : n * 128 + count]
    a_out[:, 3 * width + 128 :] = tall[0:rows, :].astype(BF16)
    b_out[:, :width] = wo[...].astype(BF16)
    b_out[:, width:] = wi[...].astype(BF16)
    c_out[...] = wc[...].astype(BF16)


def pack(lengths, permutation, vectors, bias, weights):
    rows, width = weights[0].shape
    wide = weights[4].shape[1]
    tokens = permutation.shape[1]
    assert tokens <= 3 * 128 and bias.shape[0] <= 112 and rows <= 128
    vmem = pl.BlockSpec(memory_space=pltpu.VMEM)
    return pl.pallas_call(
        pack_kernel,
        in_specs=[vmem] * 17,
        out_specs=[vmem] * 4,
        out_shape=[
            jax.ShapeDtypeStruct((rows, 3 * width + SLAB), BF16),
            jax.ShapeDtypeStruct((rows, width + wide), BF16),
            jax.ShapeDtypeStruct(weights[5].shape, BF16),
            jax.ShapeDtypeStruct((1, tokens), F32),
        ],
        scratch_shapes=[pltpu.VMEM((128, 128), F32), pltpu.VMEM((128, 128), F32)],
        compiler_params=limit("pack"),
        cost_estimate=cost(2),
        name="pack",
    )(lengths, permutation, *vectors, bias, *weights)


def head_mask(rows, head):
    lanes = lax.broadcasted_iota(jnp.int32, (rows, PAIR), 1)
    return (lanes // HEAD_DIM) == head


def attend_kernel(grid, pieces, parts, *refs):
    hidden, refs = refs[:pieces], refs[pieces:]
    part_refs, refs = refs[:parts], refs[parts:]
    own_doc, all_doc = refs[:2]
    q_out, kv_out, att_out, log_out, vec_out, bias_out, bias, weights, slab, sems = refs[2:]
    tokens = q_out.shape[0]
    keys = kv_out.shape[0]
    width = weights.shape[0]
    step = q_out.shape[1]
    group = pl.program_id(0)

    @pl.when(group == 0)
    def _():
        cols = slice(0, weights.shape[1])
        fetch(grid, part_refs, weights, sems, cols)
        bias[...] = jnp.where(own_doc[...] == all_doc[...], 0.0, -1e30).astype(F32)
        fetched(part_refs, weights, sems, cols, range(2 * grid.quads))
        slab[...] = weights[:, 3 * width : 3 * width + 128].astype(F32)
        vec_out[...] = jnp.transpose(slab[...])[0:16, :]
        rows = width // grid.devices
        count = bias_out.shape[1] // grid.devices
        for n in range(grid.devices):
            bias_out[:, n * count : (n + 1) * count] = slab[n * rows : n * rows + 1, 16 : 16 + count]

    at = pl.multiple_of(group * step, step)
    query_bias = vec_out[0:1, pl.ds(at, step)]
    value_bias = vec_out[1:2, pl.ds(at, step)]
    q_out[...] = (dot(hidden[0][...], weights[:, pl.ds(at, step)]) + query_bias).astype(BF16)
    pairs = step // PAIR
    for p in range(pieces):
        rows = slice(p * tokens, (p + 1) * tokens)
        for pair in range(pairs):
            there = pl.multiple_of(width + 2 * at + 2 * pair * PAIR, 2 * PAIR)
            both = dot(hidden[p][...], weights[:, pl.ds(there, 2 * PAIR)])
            to = 2 * pair * PAIR
            kv_out[rows, to : to + PAIR] = both[:, :PAIR].astype(BF16)
            value = both[:, PAIR:] + value_bias[:, pair * PAIR : (pair + 1) * PAIR]
            kv_out[rows, to + PAIR : to + 2 * PAIR] = value.astype(BF16)
    lane = lax.broadcasted_iota(jnp.int32, (tokens, 128), 1)
    logs = jnp.zeros((tokens, 128), F32)
    ones = jnp.ones((keys, PAIR), BF16)
    for pair in range(pairs):
        cols = slice(pair * PAIR, (pair + 1) * PAIR)
        query = q_out[:, cols]
        key = kv_out[:, 2 * pair * PAIR : (2 * pair + 1) * PAIR]
        value = jnp.concatenate([kv_out[:, (2 * pair + 1) * PAIR : (2 * pair + 2) * PAIR], ones], axis=1)
        outs = []
        for head in range(2):
            picked = jnp.where(head_mask(tokens, head), query * HEAD_DIM**-0.5, 0).astype(BF16)
            scores = times_transposed(picked, key) + bias[...]
            peak = jnp.max(scores, axis=1, keepdims=True)
            weights = jnp.exp(scores - peak).astype(BF16)
            both = dot(weights, value)
            outs.append(both[:, :PAIR] / both[:, PAIR:])
            total = peak + jnp.log(both[:, PAIR:])
            logs = jnp.where(lane == pair * 2 + head, total, logs)
        att_out[:, cols] = jnp.where(head_mask(tokens, 0), outs[0], outs[1]).astype(BF16)
    log_out[...] = logs[None]


ANY = pl.BlockSpec(memory_space=pl.ANY)
VMEM = pl.BlockSpec(memory_space=pltpu.VMEM)


def attend(grid, hidden, parts, own_doc, all_doc, wide):
    pieces = len(hidden)
    tokens, width = hidden[0].shape
    keys = pieces * tokens
    step = 256
    groups = width // step
    whole = lambda shape: pl.BlockSpec(shape, lambda g: (0, 0))
    tall = lambda rows: pl.BlockSpec((rows, step), lambda g: (0, g))
    return pl.pallas_call(
        functools.partial(attend_kernel, grid, pieces, len(parts)),
        grid=(groups,),
        in_specs=[whole(item.shape) for item in hidden]
        + [ANY] * len(parts)
        + [whole(own_doc.shape), whole(all_doc.shape)],
        out_specs=[
            tall(tokens),
            pl.BlockSpec((keys, 2 * step), lambda g: (0, g)),
            tall(tokens),
            pl.BlockSpec((1, tokens, 128), lambda g: (g, 0, 0)),
            whole((16, width)),
            whole((1, wide)),
        ],
        out_shape=[
            jax.ShapeDtypeStruct((tokens, width), BF16),
            jax.ShapeDtypeStruct((keys, 2 * width), BF16),
            jax.ShapeDtypeStruct((tokens, width), BF16),
            jax.ShapeDtypeStruct((groups, tokens, 128), F32),
            jax.ShapeDtypeStruct((16, width), F32),
            jax.ShapeDtypeStruct((1, wide), F32),
        ],
        scratch_shapes=[
            pltpu.VMEM((tokens, keys), F32),
            pltpu.VMEM((width, parts[0].shape[2]), BF16),
            pltpu.VMEM((width, 128), F32),
            pltpu.SemaphoreType.DMA((2 * grid.quads,)),
        ],
        compiler_params=limit("attend"),
        cost_estimate=cost(17),
        name="attend",
    )(*hidden, *parts, own_doc, all_doc)


def attend_back_kernel(start, q, kv, grad, att, logs, own_doc, doc, dq_out, dkv_out, sum_out, bias):
    tokens = q.shape[0]
    pair = pl.program_id(0) + start

    @pl.when(pair == start)
    def _():
        bias[...] = jnp.where(own_doc[...] == doc[...], 0.0, -1e30).astype(F32)

    lane = lax.broadcasted_iota(jnp.int32, (tokens, 128), 1)
    key, value = kv[:, :PAIR], kv[:, PAIR:]
    product = grad[...].astype(F32) * att[...].astype(F32)
    dq, dk, dv = [], 0.0, 0.0
    for head in range(2):
        mask = head_mask(tokens, head)
        query = jnp.where(mask, q[...] * HEAD_DIM**-0.5, 0).astype(BF16)
        part = jnp.where(mask, grad[...], 0).astype(BF16)
        slot = (pair % 2) * 2 + head
        log_total = jnp.sum(jnp.where(lane == slot, logs[0], 0.0), axis=1, keepdims=True)
        inner = jnp.sum(jnp.where(mask, product, 0.0), axis=1, keepdims=True)
        weights = jnp.exp(times_transposed(query, key) + bias[...] - log_total)
        back = (weights * (times_transposed(part, value) - inner)).astype(BF16)
        dq.append(dot(back, key) * HEAD_DIM**-0.5)
        dk = dk + outer_sum(back, query)
        dv = dv + outer_sum(weights.astype(BF16), part)
    dq_low = jnp.where(head_mask(tokens, 0), dq[0], dq[1]).astype(BF16)
    dq_out[...] = dq_low
    dkv_out[:, :PAIR] = dk.astype(BF16)
    dv_low = dv.astype(BF16)
    dkv_out[:, PAIR:] = dv_low
    sum_out[0:1, :] = column_sum(dq_low)
    sum_out[1:2, :] = column_sum(dv_low)


def attend_back(start, pairs, q, kv, grad, att, logs, own_doc, all_doc):
    tokens = q.shape[0]
    keys = kv.shape[0]
    short = pl.BlockSpec((tokens, PAIR), lambda g: (0, start + g))
    whole = lambda shape: pl.BlockSpec(shape, lambda g: (0, 0))
    return pl.pallas_call(
        functools.partial(attend_back_kernel, start),
        grid=(pairs,),
        in_specs=[
            short,
            pl.BlockSpec((keys, 2 * PAIR), lambda g: (0, start + g)),
            short,
            short,
            pl.BlockSpec((1, tokens, 128), lambda g: ((start + g) // 2, 0, 0)),
            whole(own_doc.shape),
            whole(all_doc.shape),
        ],
        out_specs=[
            pl.BlockSpec((tokens, PAIR), lambda g: (0, g)),
            pl.BlockSpec((keys, 2 * PAIR), lambda g: (0, g)),
            pl.BlockSpec((8, PAIR), lambda g: (0, g)),
        ],
        out_shape=[
            jax.ShapeDtypeStruct((tokens, pairs * PAIR), BF16),
            jax.ShapeDtypeStruct((keys, 2 * pairs * PAIR), BF16),
            jax.ShapeDtypeStruct((8, pairs * PAIR), F32),
        ],
        scratch_shapes=[pltpu.VMEM((tokens, keys), F32)],
        compiler_params=limit("attend_back"),
        cost_estimate=cost(11),
        name="attend_back",
    )(q, kv, grad, att, logs, own_doc, all_doc)


def interleave(key, value):
    rows, width = key.shape
    split = lambda item: item.reshape(rows, width // PAIR, 1, PAIR)
    return jnp.concatenate([split(key), split(value)], axis=2).reshape(rows, 2 * width)


def part_of(both, which):
    rows, width = both.shape
    return both.reshape(rows, width // (2 * PAIR), 2, PAIR)[:, :, which].reshape(rows, width // 2)


def row_mean(values):
    return jnp.mean(values, axis=-1, keepdims=True)


def column_sum(values):
    return jnp.sum(values.astype(F32), axis=0, keepdims=True)


def norm_back(grad_out, normed, inverse, scale_gain):
    grad_normed = grad_out * scale_gain
    inner = grad_normed - row_mean(grad_normed) - normed * row_mean(grad_normed * normed)
    return inner * inverse


def normalize(values):
    centred = values - row_mean(values)
    inverse = lax.rsqrt(row_mean(centred * centred) + EPSILON)
    return centred * inverse, inverse


def middle_kernel(grid, parts, att, hidden, cotangent, vec, b_expand, *refs):
    parts_b, parts_c, refs = refs[:parts], refs[parts : 2 * parts], refs[2 * parts :]
    result, first_out, normed_out, inverse_out, slope, second_out, low_out, keep, send, sums = refs[:10]
    wb, wc, active, staged, sem_b, sem_c, sem_out = refs[10:]
    width, wide = wb.shape[0], wc.shape[0]
    every = range(2 * grid.quads)
    chunks = [slice(n * width, (n + 1) * width) for n in range(wide // width + 1)]
    for n, cols in enumerate(chunks):
        fetch(grid, parts_b, wb, sem_b.at[n], cols)
    fetch(grid, parts_c, wc, sem_c, chunks[0])
    fetched(parts_b, wb, sem_b.at[0], chunks[0], every)
    mixed = dot(att[...], wb[:, :width]) + vec[2:3, :]
    normed, inverse = normalize(hidden[...].astype(F32) + mixed)
    normed_out[...] = normed
    inverse_out[...] = jnp.broadcast_to(inverse, inverse_out.shape)
    first = normed * vec[3:4, :] + vec[4:5, :]
    first_out[...] = first.astype(BF16)
    for n in range(wide // width):
        cols = chunks[n]
        fetched(parts_b, wb, sem_b.at[n + 1], chunks[n + 1], every)
        into = dot(first_out[...], wb[:, chunks[n + 1]]) + b_expand[:, cols]
        chance = 0.5 * (1.0 + lax.erf(into * (0.5**0.5)))
        density = jnp.exp(-0.5 * into * into) * ((2.0 * math.pi) ** -0.5)
        active[:, cols] = (into * chance).astype(BF16)
        slope[:, cols] = (chance + into * density).astype(BF16)
    fetched(parts_c, wc, sem_c, chunks[0], every)
    contracted = dot(active[...], wc[...]) + vec[5:6, :]
    normed, inverse = normalize(first + contracted)
    result[...] = (normed * vec[6:7, :] + vec[7:8, :]).astype(BF16)
    grad = cotangent[...].astype(F32)
    second = norm_back(grad, normed, inverse, vec[6:7, :])
    second_out[...] = second
    low = second.astype(BF16)
    low_out[...] = low
    sums[...] = jnp.zeros_like(sums)
    sums[5:6, :] = column_sum(low)
    sums[6:7, :] = column_sum(grad * normed)
    sums[7:8, :] = column_sum(grad)
    blocks = width // keep.shape[1]
    for n in range(wide // width):
        staged[chunks[n], :] = outer_sum(active[:, chunks[n]], low).astype(BF16)
        store_blocks(grid, staged, n * blocks, blocks, chunks[0], keep, send, sem_out)
    stored(grid, staged, every, chunks[0], keep, sem_out)


def middle(grid, att, hidden, cotangent, vec, b_expand, parts_b, parts_c):
    tokens, width = hidden.shape
    wide = b_expand.shape[1]
    blocks = jax.ShapeDtypeStruct((grid.quads,) + parts_c[0].shape[1:], BF16)
    return pl.pallas_call(
        functools.partial(middle_kernel, grid, len(parts_b)),
        in_specs=[VMEM] * 5 + [ANY] * (2 * len(parts_b)),
        out_specs=[VMEM] * 7 + [ANY] * 2 + [VMEM],
        out_shape=[
            jax.ShapeDtypeStruct((tokens, width), BF16),
            jax.ShapeDtypeStruct((tokens, width), BF16),
            jax.ShapeDtypeStruct((tokens, width), F32),
            jax.ShapeDtypeStruct((tokens, 128), F32),
            jax.ShapeDtypeStruct((tokens, wide), BF16),
            jax.ShapeDtypeStruct((tokens, width), F32),
            jax.ShapeDtypeStruct((tokens, width), BF16),
            blocks,
            blocks,
            jax.ShapeDtypeStruct((8, width), F32),
        ],
        scratch_shapes=[
            pltpu.VMEM((width, width + wide), BF16),
            pltpu.VMEM((wide, width), BF16),
            pltpu.VMEM((tokens, wide), BF16),
            pltpu.VMEM((wide, width), BF16),
            pltpu.SemaphoreType.DMA((wide // width + 1, 2 * grid.quads)),
            pltpu.SemaphoreType.DMA((2 * grid.quads,)),
            pltpu.SemaphoreType.DMA((2 * grid.quads,)),
        ],
        compiler_params=limit("middle"),
        cost_estimate=cost(20),
        name="middle",
    )(att, hidden, cotangent, vec, b_expand, *parts_b, *parts_c)


def dense_back_kernel(grid, parts, att, first, normed, inverse, slope, second, low, vec, *refs):
    parts_b, parts_c, refs = refs[:parts], refs[parts : 2 * parts], refs[2 * parts :]
    grad_sum, att_back, keep, send, sums, bias_sum = refs[:6]
    wb, wc, back, staged, sem_b, sem_c, sem_out = refs[6:]
    width, wide = wb.shape[0], wc.shape[0]
    every = range(2 * grid.quads)
    chunks = [slice(n * width, (n + 1) * width) for n in range(wide // width + 1)]
    per_chunk = len(every) * width // wide
    fetch(grid, parts_c, wc, sem_c, chunks[0])
    fetch(grid, parts_b, wb, sem_b, slice(0, wb.shape[1]))
    for n in range(wide // width):
        cols = chunks[n]
        fetched(parts_c, wc, sem_c, chunks[0], range(n * per_chunk, (n + 1) * per_chunk))
        piece = (times_transposed(low[...], wc[cols, :]) * slope[:, cols].astype(F32)).astype(BF16)
        back[:, cols] = piece
        bias_sum[:, cols] = column_sum(piece)
    fetched(parts_b, wb, sem_b, slice(0, wb.shape[1]), every)
    grad_first = second[...] + times_transposed(back[...], wb[:, width:])
    grad = norm_back(grad_first, normed[...], inverse[:, 0:1], vec[3:4, :])
    grad_sum[...] = grad
    mixed = grad.astype(BF16)
    att_back[...] = times_transposed(mixed, wb[:, :width]).astype(BF16)
    sums[...] = jnp.zeros_like(sums)
    sums[2:3, :] = column_sum(mixed)
    sums[3:4, :] = column_sum(grad_first * normed[...])
    sums[4:5, :] = column_sum(grad_first)
    for n, cols in enumerate(chunks):
        if n == 0:
            staged[:, cols] = outer_sum(att[...], mixed).astype(BF16)
        else:
            staged[:, cols] = outer_sum(first[...], back[:, chunks[n - 1]]).astype(BF16)
        store_blocks(grid, staged, 0, len(every), cols, keep, send, sem_out.at[n])
    for n, cols in enumerate(chunks):
        stored(grid, staged, every, cols, keep, sem_out.at[n])


def dense_back(grid, att, first, normed, inverse, slope, second, low, vec, parts_b, parts_c):
    tokens, width = att.shape
    wide = slope.shape[1]
    blocks = jax.ShapeDtypeStruct((grid.quads,) + parts_b[0].shape[1:], BF16)
    return pl.pallas_call(
        functools.partial(dense_back_kernel, grid, len(parts_b)),
        in_specs=[VMEM] * 8 + [ANY] * (2 * len(parts_b)),
        out_specs=[VMEM] * 2 + [ANY] * 2 + [VMEM] * 2,
        out_shape=[
            jax.ShapeDtypeStruct((tokens, width), F32),
            jax.ShapeDtypeStruct((tokens, width), BF16),
            blocks,
            blocks,
            jax.ShapeDtypeStruct((8, width), F32),
            jax.ShapeDtypeStruct((1, wide), F32),
        ],
        scratch_shapes=[
            pltpu.VMEM((width, width + wide), BF16),
            pltpu.VMEM((wide, width), BF16),
            pltpu.VMEM((tokens, wide), BF16),
            pltpu.VMEM((width, width + wide), BF16),
            pltpu.SemaphoreType.DMA((2 * grid.quads,)),
            pltpu.SemaphoreType.DMA((2 * grid.quads,)),
            pltpu.SemaphoreType.DMA((wide // width + 1, 2 * grid.quads)),
        ],
        compiler_params=limit("dense_back"),
        cost_estimate=cost(20),
        name="dense_back",
    )(att, first, normed, inverse, slope, second, low, vec, *parts_b, *parts_c)


def input_back_kernel(grid, parts, grad_sum, dq0, dq1, dkv0, dkv1, *refs):
    part_refs, outs = refs[:parts], refs[parts:-3]
    weights, total, sems = refs[-3:]
    tokens = grad_sum.shape[0]
    width = weights.shape[0]
    half = dkv0.shape[1]
    cols = slice(0, weights.shape[1])
    every = range(2 * grid.quads)
    fetch(grid, part_refs, weights, sems, cols)
    fetched(part_refs, weights, sems, cols, every)
    step = 256
    for n in range(width // step):
        to = slice(n * step, (n + 1) * step)
        total[...] = times_transposed(dkv0[...], weights[to, width : width + half]) + times_transposed(
            dkv1[...], weights[to, width + half : 3 * width]
        )
        for piece in range(len(outs)):
            back = total[piece * tokens : (piece + 1) * tokens, :]
            if piece == 0:
                back = back + times_transposed(dq0[...], weights[to, : half // 2])
                back = back + times_transposed(dq1[...], weights[to, half // 2 : width])
                back = back + grad_sum[:, to]
            outs[piece][:, to] = back.astype(outs[piece].dtype)


def input_back(grid, grad_sum, first_part, last_part, parts):
    tokens, width = grad_sum.shape
    return pl.pallas_call(
        functools.partial(input_back_kernel, grid, len(parts)),
        in_specs=[VMEM] * 5 + [ANY] * len(parts),
        out_specs=[VMEM] * grid.bands,
        out_shape=[jax.ShapeDtypeStruct((tokens, width), F32)]
        + [jax.ShapeDtypeStruct((tokens, width), BF16)] * (grid.bands - 1),
        scratch_shapes=[
            pltpu.VMEM((width, parts[0].shape[2]), BF16),
            pltpu.VMEM((grid.bands * tokens, 256), F32),
            pltpu.SemaphoreType.DMA((2 * grid.quads,)),
        ],
        compiler_params=limit("input_back"),
        cost_estimate=cost(9),
        name="input_back",
    )(grad_sum, first_part[0], last_part[0], first_part[1], last_part[1], *parts)


def weight_back_kernel(grid, pieces, *refs):
    hidden, refs = refs[:pieces], refs[pieces:]
    dq0, dq1, dkv0, dkv1, sum0, sum1, sum2, sum3, bias_sum, keep, send = refs[:11]
    every, staged, stage, slab, sem_in, sem_out = refs[11:]
    tokens, width = hidden[0].shape
    half = dkv0.shape[1]
    blocks = 2 * grid.quads
    copies = [
        pltpu.make_async_copy(hidden[n], every.at[pl.ds(n * tokens, tokens), :], sem_in.at[n])
        for n in range(pieces)
    ]
    for copy in copies:
        copy.start()
    for copy in copies:
        copy.wait()
    chunks = [slice(n * width, (n + 1) * width) for n in range(3)] + [slice(3 * width, 3 * width + SLAB)]
    for n, item in enumerate((dkv0, dkv1)):
        staged[:, chunks[1 + n]] = outer_sum(every[...], item[...]).astype(BF16)
        store_blocks(grid, staged, 0, blocks, chunks[1 + n], keep, send, sem_out.at[1 + n])
    for n, item in enumerate((dq0, dq1)):
        cols = slice(n * half // 2, (n + 1) * half // 2)
        staged[:, cols] = outer_sum(every[0:tokens, :], item[...]).astype(BF16)
    store_blocks(grid, staged, 0, blocks, chunks[0], keep, send, sem_out.at[0])
    stage[...] = jnp.zeros_like(stage)
    stage[0:8, :] = sum2[...] + sum3[...]
    for n, item in enumerate((sum0, sum1)):
        stage[0:2, n * half // 2 : (n + 1) * half // 2] = item[0:2, :]
    slab[:, :128] = jnp.transpose(stage[...])
    slab[:, 128:] = jnp.zeros((width, SLAB - 128), F32)
    rows = width // grid.devices
    count = bias_sum.shape[1] // grid.devices
    for n in range(grid.devices):
        slab[n * rows : n * rows + 1, 16 : 16 + count] = bias_sum[:, n * count : (n + 1) * count]
    staged[:, chunks[3]] = slab[...].astype(BF16)
    store_blocks(grid, staged, 0, blocks, chunks[3], keep, send, sem_out.at[3])
    for n, cols in enumerate(chunks):
        stored(grid, staged, range(blocks), cols, keep, sem_out.at[n])


def weight_back(grid, hidden, first_part, last_part, sums, bias_sum):
    pieces = len(hidden)
    tokens, width = hidden[0].shape
    tall = width // (2 * grid.quads)
    blocks = jax.ShapeDtypeStruct((grid.quads, tall, 3 * width + SLAB), BF16)
    return pl.pallas_call(
        functools.partial(weight_back_kernel, grid, pieces),
        in_specs=[ANY] * pieces + [VMEM] * 9,
        out_specs=[ANY] * 2,
        out_shape=[blocks, blocks],
        scratch_shapes=[
            pltpu.VMEM((pieces * tokens, width), BF16),
            pltpu.VMEM((width, 3 * width + SLAB), BF16),
            pltpu.VMEM((128, width), F32),
            pltpu.VMEM((width, SLAB), F32),
            pltpu.SemaphoreType.DMA((pieces,)),
            pltpu.SemaphoreType.DMA((4, 2 * grid.quads)),
        ],
        compiler_params=limit("weight_back"),
        cost_estimate=cost(11),
        name="weight_back",
    )(
        *hidden,
        first_part[0],
        last_part[0],
        first_part[1],
        last_part[1],
        first_part[2],
        last_part[2],
        *sums,
        bias_sum,
    )


def add_kernel(left, right, later, out):
    out[...] = (left[...].astype(F32) + right[...].astype(F32)).astype(out.dtype)


def add_rows(left, right, later):
    return pl.pallas_call(
        add_kernel,
        in_specs=[VMEM, VMEM, ANY],
        out_specs=VMEM,
        out_shape=jax.ShapeDtypeStruct(left.shape, left.dtype),
        cost_estimate=cost(30),
        name="add_rows",
    )(left, right, later)


def per_device(
    grid,
    hidden_in,
    lengths,
    permutation,
    query_weight,
    query_bias,
    key_weight,
    value_weight,
    value_bias,
    mix_weight,
    mix_bias,
    first_gain,
    first_shift,
    expand_weight,
    expand_bias,
    contract_weight,
    contract_bias,
    second_gain,
    second_shift,
    cotangent,
):
    tokens, width = hidden_in.shape
    wide = contract_weight.shape[0] * grid.devices
    rows = query_weight.shape[0]
    bands = grid.bands

    vectors = [query_bias, value_bias, mix_bias, first_gain, first_shift, contract_bias, second_gain, second_shift]
    weights = [query_weight, key_weight, value_weight, mix_weight, expand_weight, contract_weight]
    shard_a, shard_b, shard_c, doc = pack(lengths, permutation, vectors, expand_bias, weights)

    pieces_a = z_direct(grid, shard_a)
    gather_a = Gather(grid, pieces_a)
    gather_a.near_step()
    pieces_b = z_direct(grid, after(shard_b, *pieces_a))
    pieces_c = z_direct(grid, after(shard_c, *pieces_a, gather_a.near_all))
    gather_b, gather_c = Gather(grid, pieces_b), Gather(grid, pieces_c)
    messages = [hidden_in]
    messages.append(grid.along_z(after(hidden_in, *pieces_b, *pieces_c, gather_a.near_all), 1))
    gather_a.far_step()
    gather_b.near_step()
    gather_c.near_step()
    parts_a = gather_a.core_step(messages[1])
    gather_b.far_step(messages[1], *gather_a.far_all)
    messages.append(grid.along_z(messages[1], 1))
    gather_c.far_step(messages[1], *gather_a.far_all)
    parts_b = gather_b.core_step(messages[2])
    for step in range(3, bands):
        messages.append(grid.along_z(messages[-1], 1))
    messages[0] = after(messages[0], gather_c.near_all, gather_b.near_all)

    docs_of = [doc] + [
        item[0:3, 3 * width + 128 :].astype(F32).reshape(1, 3 * 128)[:, :tokens] for item in pieces_a[1:]
    ]
    all_doc = jnp.concatenate(docs_of, axis=1)
    own_doc = doc.reshape(tokens, 1)
    q, kv, attended, logs, vec, b_expand = attend(grid, messages, parts_a, own_doc, all_doc, wide)
    gather_c.far_all = after(gather_c.far_all, attended)
    parts_c = gather_c.core_step()
    result, first, normed, inverse, slope, second, low, keep, send, sums_two = middle(
        grid, attended, hidden_in, cotangent, vec, b_expand, parts_b, parts_c
    )
    sum_c = Sum(grid, keep, send)
    grad_sum, attended_back, keep, send, sums_one, d_b_expand = dense_back(
        grid, attended, first, normed, inverse, slope, second, low, vec, parts_b, parts_c
    )
    sum_c.core_step(grad_sum)
    sum_b = Sum(grid, keep, send)
    attended_back = after(attended_back, sum_c.send)

    pairs = width // PAIR
    half = pairs // 2
    first_part = attend_back(0, half, q, kv, attended_back, attended, logs, own_doc, all_doc)
    sum_c.far_step(first_part)
    sum_b.core_step(sum_c.send)
    attended_back = after(attended_back, sum_b.send, sum_c.send)
    last_part = attend_back(half, pairs - half, q, kv, attended_back, attended, logs, own_doc, all_doc)
    sum_c.near_step(last_part)
    sum_b.far_step(sum_c.send)
    last_part = after(last_part, sum_c.send, sum_b.send)
    backs = input_back(grid, grad_sum, first_part, last_part, parts_a)
    sent = backs[bands - 1]
    d_contract = sum_c.z_step(sent)
    last_part = after(last_part, backs, d_contract)
    keep, send = weight_back(grid, messages, first_part, last_part, (sums_two, sums_one), d_b_expand)
    sum_a = Sum(grid, keep, send)
    for piece in range(bands - 1, 0, -1):
        got = grid.along_z(sent, -1)
        if piece == bands - 1:
            sent = add_rows(backs[piece - 1], got, keep)
            sum_a.core_step(sent)
            sum_b.near_step(sum_a.send)
        elif piece > 1:
            sent = add_rows(backs[piece - 1], got, sum_b.send[0])
            if piece == bands - 2:
                sum_a.far_step(sent)
        else:
            last = got
    d_b = sum_b.z_step(sum_a.send)
    sum_a.near_step(d_b)
    grad_input = after(backs[0], sum_a.send) + last.astype(F32)
    d_a = sum_a.z_step()
    slab = d_a[:, 3 * width :]
    small = [slab[:, n] for n in range(8)]
    d_both = d_a[:, width : 3 * width]
    return (
        result,
        grad_input.astype(BF16),
        d_a[:, :width],
        small[0],
        part_of(d_both, 0),
        part_of(d_both, 1),
        small[1],
        d_b[:, :width],
        small[2],
        small[3],
        small[4],
        d_b[:, width:],
        slab[0, 16 : 16 + expand_bias.shape[0]],
        d_contract,
        small[5],
        small[6],
        small[7],
    )


def solution(mesh):
    grid = Grid(mesh.shape["page"], mesh.shape["band"])
    matrix, vector = P(AXES, None), P(AXES)
    parameters = (
        matrix,
        vector,
        matrix,
        matrix,
        vector,
        matrix,
        vector,
        vector,
        vector,
        matrix,
        vector,
        matrix,
        vector,
        vector,
        vector,
    )
    return jax.shard_map(
        functools.partial(per_device, grid),
        mesh=mesh,
        in_specs=(matrix, P("page", None), P("page", "band")) + parameters + (matrix,),
        out_specs=(matrix, matrix) + parameters,
        check_vma=False,
    )
```

```python
import functools
import itertools
import math

import jax
import jax.numpy as jnp
from jax import lax
from jax.experimental import pallas as pl
from jax.experimental.pallas import tpu as pltpu
from jax.sharding import PartitionSpec as P

HEAD_DIM = 64
PAIR = 2 * HEAD_DIM
EPSILON = 1e-12
AXES = ("page", "band")
SLAB = 256
BF16, F32 = jnp.bfloat16, jnp.float32
COSTS = {
    "pack": 1,
    "attend": 1,
    "middle": 8,
    "dense_back": 10,
    "attend_back": 5,
    "input_back": 4,
    "weight_back": 5,
    "add_rows": 15,
}
LIMITS = {
    "pack": 60,
    "attend": 52,
    "middle": 36,
    "dense_back": 36,
    "attend_back": 54,
    "input_back": 32,
    "weight_back": 32,
}


def limit(kernel):
    return pltpu.CompilerParams(vmem_limit_bytes=LIMITS[kernel] * 2**20)


def cost(kernel):
    return pl.CostEstimate(flops=int(COSTS[kernel] * 1.1e9), bytes_accessed=1024, transcendentals=0)


def dot(left, right):
    return lax.dot_general(left, right, (((1,), (0,)), ((), ())), preferred_element_type=F32)


def times_transposed(left, right):
    return lax.dot_general(left, right, (((1,), (1,)), ((), ())), preferred_element_type=F32)


def outer_sum(left, right):
    return lax.dot_general(left, right, (((0,), (0,)), ((), ())), preferred_element_type=F32)


class Grid:
    def __init__(self, pages, bands):
        self.side = math.isqrt(pages // 2)
        assert self.side * self.side * 2 == pages
        self.bands = bands
        self.devices = pages * bands
        self.quads = self.side * self.side

    def linear(self, i, j, c, z):
        return ((i * self.side + j) * 2 + c) * self.bands + z

    def permute(self, array, move):
        side, bands = self.side, self.bands
        pairs = []
        for i, j, c, z in itertools.product(range(side), range(side), range(2), range(bands)):
            ti, tj, tc, tz = move(i, j, c, z)
            pairs.append((self.linear(i, j, c, z), self.linear(ti % side, tj % side, tc, tz % bands)))
        return lax.ppermute(array, AXES, pairs)

    def along_z(self, array, step):
        return self.permute(array, lambda i, j, c, z: (i, j, c, z + step))

    def near(self, array, step):
        return self.permute(
            array, lambda i, j, c, z: (i, j + step, c, z) if c == 0 else (i + step, j, c, z)
        )

    def far(self, array, step):
        return self.permute(
            array, lambda i, j, c, z: (i + step, j, c, z) if c == 0 else (i, j + step, c, z)
        )

    def across(self, array):
        return self.permute(array, lambda i, j, c, z: (i, j, 1 - c, z))

    def place(self):
        page, z = lax.axis_index("page"), lax.axis_index("band")
        return page // (2 * self.side), (page // 2) % self.side, page % 2, z


def after(value, *others):
    return lax.optimization_barrier((value, others))[0]


def z_direct(grid, shard):
    return [shard] + [grid.along_z(shard, step) for step in range(1, grid.bands)]


class Gather:
    def __init__(self, grid, pieces):
        self.grid = grid
        rows, width = pieces[0].shape
        z = lax.axis_index("band")
        block = jnp.zeros((grid.bands, rows, width), pieces[0].dtype)
        for step, piece in enumerate(pieces):
            block = lax.dynamic_update_slice(block, piece[None], ((z - step) % grid.bands, 0, 0))
        self.block = block.reshape(grid.bands * rows, width)

    def near_step(self, *pins):
        block = after(self.block, *pins)
        got = [self.grid.near(block, step) for step in range(1, self.grid.side)]
        self.near_all = jnp.stack([self.block] + got)

    def far_step(self, *pins):
        near_all = after(self.near_all, *pins)
        self.far_all = [self.grid.far(near_all, step) for step in range(1, self.grid.side)]

    def core_step(self, *pins):
        parts = [self.near_all] + self.far_all
        first = self.grid.across(after(self.near_all, *pins))
        return parts + [first] + [self.grid.across(item) for item in self.far_all]


def fetch(grid, parts, whole, sems, cols):
    i, j, c, _ = grid.place()
    tall = parts[0].shape[1]
    for d in range(2):
        core = (c + d) % 2
        for a in range(grid.side):
            for b in range(grid.side):
                di = jnp.where(core == 0, a, b)
                dj = jnp.where(core == 0, b, a)
                up = (i - di + grid.side) % grid.side
                left = (j - dj + grid.side) % grid.side
                index = (up * grid.side + left) * 2 + core
                pltpu.make_async_copy(
                    parts[d * grid.side + a].at[b, :, cols],
                    whole.at[pl.ds(pl.multiple_of(index * tall, 8), tall), cols],
                    sems.at[index],
                ).start()


def fetched(parts, whole, sems, cols, blocks):
    tall = parts[0].shape[1]
    for n in blocks:
        pltpu.make_async_copy(
            parts[0].at[0, :, cols], whole.at[pl.ds(n * tall, tall), cols], sems.at[n]
        ).wait()


def store_blocks(grid, staged, first, blocks, cols, keep, send, sems):
    i, j, c, _ = grid.place()
    tall = keep.shape[1]
    for n in range(blocks):
        block = first + n
        core = block % 2
        ti, tj = block // (2 * grid.side), (block // 2) % grid.side
        di = (ti - i + grid.side) % grid.side
        dj = (tj - j + grid.side) % grid.side
        slot = di * grid.side + dj if core == 0 else dj * grid.side + di
        source = staged.at[pl.ds(block * tall, tall), cols]

        @pl.when(c == core)
        def _():
            pltpu.make_async_copy(source, keep.at[slot, :, cols], sems.at[block]).start()

        @pl.when(c != core)
        def _():
            pltpu.make_async_copy(source, send.at[slot, :, cols], sems.at[block]).start()


def stored(grid, staged, blocks, cols, keep, sems):
    tall = keep.shape[1]
    for block in blocks:
        source = staged.at[pl.ds(block * tall, tall), cols]
        pltpu.make_async_copy(source, keep.at[0, :, cols], sems.at[block]).wait()


class Sum:
    def __init__(self, grid, keep, send):
        self.grid, self.send = grid, send
        self.terms = [keep]

    def total(self, at):
        result = self.terms[0][at].astype(F32)
        for item in self.terms[1:]:
            result = result + item[at].astype(F32)
        return result

    def move_core(self):
        self.got = self.grid.across(self.send)

    def add_core(self, *pins):
        side = self.grid.side
        self.terms = after(self.terms, *pins) + [self.got]
        self.send = [self.total(slice(a * side, (a + 1) * side)).astype(BF16) for a in range(1, side)]

    def move_far(self):
        self.got = [self.grid.far(item, a) for a, item in enumerate(self.send, 1)]

    def add_far(self, *pins):
        self.terms = after(self.terms, *pins) + self.got
        self.send = [self.total(b).astype(BF16) for b in range(1, self.grid.side)]

    def move_near(self):
        self.got = [self.grid.near(item, b)[None] for b, item in enumerate(self.send, 1)]

    def add_near(self, *pins):
        bands = self.grid.bands
        self.terms = after(self.terms, *pins) + self.got
        own = self.total(0)
        own = own.reshape(bands, own.shape[0] // bands, own.shape[1])
        z = lax.axis_index("band")
        self.own = lax.dynamic_index_in_dim(own, z, 0, False)
        self.send = [
            lax.dynamic_index_in_dim(own, (z + step) % bands, 0, False).astype(BF16)
            for step in range(1, bands)
        ]

    def move_z(self):
        self.got = [self.grid.along_z(item, step) for step, item in enumerate(self.send, 1)]

    def add_z(self, *pins):
        own = after(self.own, *pins)
        for item in self.got:
            own = own + item.astype(F32)
        return own

    def core_step(self, *pins):
        self.move_core()
        self.add_core(*pins)

    def far_step(self, *pins):
        self.move_far()
        self.add_far(*pins)

    def near_step(self, *pins):
        self.move_near()
        self.add_near(*pins)

    def z_step(self, *pins):
        self.move_z()
        return self.add_z(*pins)


def pack_kernel(lengths, permutation, *refs):
    vectors, bias = refs[:8], refs[8]
    wq, wk, wv, wo, wi, wc = refs[9:15]
    a_out, b_out, c_out, doc_out = refs[15:19]
    stage, tall = refs[19:]
    rows, width = wq.shape
    docs = lengths.shape[1]
    tokens = permutation.shape[1]
    earlier = lax.broadcasted_iota(jnp.int32, (docs, docs), 1) <= lax.broadcasted_iota(
        jnp.int32, (docs, docs), 0
    )
    ends = jnp.sum(jnp.where(earlier, lengths[...], 0).astype(F32), axis=1, keepdims=True)
    marks = jnp.sum(
        jnp.where(permutation[...].astype(F32) >= ends, 1.0, 0.0), axis=0, keepdims=True
    )
    doc_out[...] = marks
    a_out[:, :width] = wq[...].astype(BF16)
    for pair in range(width // PAIR):
        at = width + 2 * pair * PAIR
        cols = slice(pair * PAIR, (pair + 1) * PAIR)
        a_out[:, at : at + PAIR] = wk[:, cols].astype(BF16)
        a_out[:, at + PAIR : at + 2 * PAIR] = wv[:, cols].astype(BF16)
    stage[...] = jnp.zeros_like(stage)
    for n, item in enumerate(vectors):
        stage[n : n + 1, 0:rows] = item[...].reshape(1, rows)
    tall[...] = jnp.transpose(stage[...])
    tall[0:1, 16 : 16 + bias.shape[0]] = bias[...].reshape(1, bias.shape[0])
    a_out[:, 3 * width : 3 * width + 128] = tall[0:rows, :].astype(BF16)
    tall[...] = jnp.zeros_like(tall)
    for n in range(3):
        count = min(128, tokens - n * 128)
        tall[n : n + 1, 0:count] = marks[:, n * 128 : n * 128 + count]
    a_out[:, 3 * width + 128 :] = tall[0:rows, :].astype(BF16)
    b_out[:, :width] = wo[...].astype(BF16)
    b_out[:, width:] = wi[...].astype(BF16)
    c_out[...] = wc[...].astype(BF16)


def pack(lengths, permutation, vectors, bias, weights):
    rows, width = weights[0].shape
    wide = weights[4].shape[1]
    tokens = permutation.shape[1]
    assert tokens <= 3 * 128 and bias.shape[0] <= 112 and rows <= 128
    vmem = pl.BlockSpec(memory_space=pltpu.VMEM)
    return pl.pallas_call(
        pack_kernel,
        in_specs=[vmem] * 17,
        out_specs=[vmem] * 4,
        out_shape=[
            jax.ShapeDtypeStruct((rows, 3 * width + SLAB), BF16),
            jax.ShapeDtypeStruct((rows, width + wide), BF16),
            jax.ShapeDtypeStruct(weights[5].shape, BF16),
            jax.ShapeDtypeStruct((1, tokens), F32),
        ],
        scratch_shapes=[pltpu.VMEM((128, 128), F32), pltpu.VMEM((128, 128), F32)],
        compiler_params=limit("pack"),
        cost_estimate=cost("pack"),
        name="pack",
    )(lengths, permutation, *vectors, bias, *weights)


def head_mask(rows, head):
    lanes = lax.broadcasted_iota(jnp.int32, (rows, PAIR), 1)
    return (lanes // HEAD_DIM) == head


def attend_kernel(grid, pieces, parts, *refs):
    hidden, refs = refs[:pieces], refs[pieces:]
    part_refs, refs = refs[:parts], refs[parts:]
    own_doc, all_doc = refs[:2]
    q_out, kv_out, att_out, log_out, vec_out, bias_out, bias, weights, slab, sems = refs[2:]
    tokens = q_out.shape[0]
    keys = kv_out.shape[0]
    width = weights.shape[0]
    step = q_out.shape[1]
    group = pl.program_id(0)

    groups = width // step
    every = range(2 * grid.quads)
    slab_cols = slice(3 * width, weights.shape[1])

    def columns(n):
        first = slice(n * step, (n + 1) * step)
        return first, slice(width + 2 * n * step, width + 2 * (n + 1) * step)

    @pl.when(group == 0)
    def _():
        fetch(grid, part_refs, weights, sems.at[0], slab_cols)
        for n in range(groups):
            for m, cols in enumerate(columns(n)):
                fetch(grid, part_refs, weights, sems.at[1 + 2 * n + m], cols)
        bias[...] = jnp.where(own_doc[...] == all_doc[...], 0.0, -1e30).astype(F32)
        fetched(part_refs, weights, sems.at[0], slab_cols, every)
        slab[...] = weights[:, 3 * width : 3 * width + 128].astype(F32)
        vec_out[...] = jnp.transpose(slab[...])[0:16, :]
        rows = width // grid.devices
        count = bias_out.shape[1] // grid.devices
        for n in range(grid.devices):
            bias_out[:, n * count : (n + 1) * count] = slab[n * rows : n * rows + 1, 16 : 16 + count]

    for n in range(groups):

        @pl.when(group == n)
        def _():
            for m, cols in enumerate(columns(n)):
                fetched(part_refs, weights, sems.at[1 + 2 * n + m], cols, every)

    at = pl.multiple_of(group * step, step)
    query_bias = vec_out[0:1, pl.ds(at, step)]
    value_bias = vec_out[1:2, pl.ds(at, step)]
    q_out[...] = (dot(hidden[0][...], weights[:, pl.ds(at, step)]) + query_bias).astype(BF16)
    pairs = step // PAIR
    for p in range(pieces):
        rows = slice(p * tokens, (p + 1) * tokens)
        for pair in range(pairs):
            there = pl.multiple_of(width + 2 * at + 2 * pair * PAIR, 2 * PAIR)
            both = dot(hidden[p][...], weights[:, pl.ds(there, 2 * PAIR)])
            to = 2 * pair * PAIR
            kv_out[rows, to : to + PAIR] = both[:, :PAIR].astype(BF16)
            value = both[:, PAIR:] + value_bias[:, pair * PAIR : (pair + 1) * PAIR]
            kv_out[rows, to + PAIR : to + 2 * PAIR] = value.astype(BF16)
    lane = lax.broadcasted_iota(jnp.int32, (tokens, 128), 1)
    logs = jnp.zeros((tokens, 128), F32)
    ones = jnp.ones((keys, PAIR), BF16)
    for pair in range(pairs):
        cols = slice(pair * PAIR, (pair + 1) * PAIR)
        query = q_out[:, cols]
        key = kv_out[:, 2 * pair * PAIR : (2 * pair + 1) * PAIR]
        value = jnp.concatenate([kv_out[:, (2 * pair + 1) * PAIR : (2 * pair + 2) * PAIR], ones], axis=1)
        outs = []
        for head in range(2):
            picked = jnp.where(head_mask(tokens, head), query * HEAD_DIM**-0.5, 0).astype(BF16)
            scores = times_transposed(picked, key) + bias[...]
            peak = jnp.max(scores, axis=1, keepdims=True)
            weights = jnp.exp(scores - peak).astype(BF16)
            both = dot(weights, value)
            outs.append(both[:, :PAIR] / both[:, PAIR:])
            total = peak + jnp.log(both[:, PAIR:])
            logs = jnp.where(lane == pair * 2 + head, total, logs)
        att_out[:, cols] = jnp.where(head_mask(tokens, 0), outs[0], outs[1]).astype(BF16)
    log_out[...] = logs[None]


ANY = pl.BlockSpec(memory_space=pl.ANY)
VMEM = pl.BlockSpec(memory_space=pltpu.VMEM)


def attend(grid, hidden, parts, own_doc, all_doc, wide):
    pieces = len(hidden)
    tokens, width = hidden[0].shape
    keys = pieces * tokens
    step = 256
    groups = width // step
    whole = lambda shape: pl.BlockSpec(shape, lambda g: (0, 0))
    tall = lambda rows: pl.BlockSpec((rows, step), lambda g: (0, g))
    return pl.pallas_call(
        functools.partial(attend_kernel, grid, pieces, len(parts)),
        grid=(groups,),
        in_specs=[whole(item.shape) for item in hidden]
        + [ANY] * len(parts)
        + [whole(own_doc.shape), whole(all_doc.shape)],
        out_specs=[
            tall(tokens),
            pl.BlockSpec((keys, 2 * step), lambda g: (0, g)),
            tall(tokens),
            pl.BlockSpec((1, tokens, 128), lambda g: (g, 0, 0)),
            whole((16, width)),
            whole((1, wide)),
        ],
        out_shape=[
            jax.ShapeDtypeStruct((tokens, width), BF16),
            jax.ShapeDtypeStruct((keys, 2 * width), BF16),
            jax.ShapeDtypeStruct((tokens, width), BF16),
            jax.ShapeDtypeStruct((groups, tokens, 128), F32),
            jax.ShapeDtypeStruct((16, width), F32),
            jax.ShapeDtypeStruct((1, wide), F32),
        ],
        scratch_shapes=[
            pltpu.VMEM((tokens, keys), F32),
            pltpu.VMEM((width, parts[0].shape[2]), BF16),
            pltpu.VMEM((width, 128), F32),
            pltpu.SemaphoreType.DMA((1 + 2 * groups, 2 * grid.quads)),
        ],
        compiler_params=limit("attend"),
        cost_estimate=cost("attend"),
        name="attend",
    )(*hidden, *parts, own_doc, all_doc)


def attend_back_kernel(start, q, kv, grad, att, logs, own_doc, doc, dq_out, dkv_out, sum_out, bias):
    tokens = q.shape[0]
    pair = pl.program_id(0) + start

    @pl.when(pair == start)
    def _():
        bias[...] = jnp.where(own_doc[...] == doc[...], 0.0, -1e30).astype(F32)

    lane = lax.broadcasted_iota(jnp.int32, (tokens, 128), 1)
    key, value = kv[:, :PAIR], kv[:, PAIR:]
    product = grad[...].astype(F32) * att[...].astype(F32)
    dq, dk, dv = [], 0.0, 0.0
    for head in range(2):
        mask = head_mask(tokens, head)
        query = jnp.where(mask, q[...] * HEAD_DIM**-0.5, 0).astype(BF16)
        part = jnp.where(mask, grad[...], 0).astype(BF16)
        slot = (pair % 2) * 2 + head
        log_total = jnp.sum(jnp.where(lane == slot, logs[0], 0.0), axis=1, keepdims=True)
        inner = jnp.sum(jnp.where(mask, product, 0.0), axis=1, keepdims=True)
        weights = jnp.exp(times_transposed(query, key) + bias[...] - log_total)
        back = (weights * (times_transposed(part, value) - inner)).astype(BF16)
        dq.append(dot(back, key) * HEAD_DIM**-0.5)
        dk = dk + outer_sum(back, query)
        dv = dv + outer_sum(weights.astype(BF16), part)
    dq_low = jnp.where(head_mask(tokens, 0), dq[0], dq[1]).astype(BF16)
    dq_out[...] = dq_low
    dkv_out[:, :PAIR] = dk.astype(BF16)
    dv_low = dv.astype(BF16)
    dkv_out[:, PAIR:] = dv_low
    sum_out[0:1, :] = column_sum(dq_low)
    sum_out[1:2, :] = column_sum(dv_low)


def attend_back(start, pairs, q, kv, grad, att, logs, own_doc, all_doc):
    tokens = q.shape[0]
    keys = kv.shape[0]
    short = pl.BlockSpec((tokens, PAIR), lambda g: (0, start + g))
    whole = lambda shape: pl.BlockSpec(shape, lambda g: (0, 0))
    return pl.pallas_call(
        functools.partial(attend_back_kernel, start),
        grid=(pairs,),
        in_specs=[
            short,
            pl.BlockSpec((keys, 2 * PAIR), lambda g: (0, start + g)),
            short,
            short,
            pl.BlockSpec((1, tokens, 128), lambda g: ((start + g) // 2, 0, 0)),
            whole(own_doc.shape),
            whole(all_doc.shape),
        ],
        out_specs=[
            pl.BlockSpec((tokens, PAIR), lambda g: (0, g)),
            pl.BlockSpec((keys, 2 * PAIR), lambda g: (0, g)),
            pl.BlockSpec((8, PAIR), lambda g: (0, g)),
        ],
        out_shape=[
            jax.ShapeDtypeStruct((tokens, pairs * PAIR), BF16),
            jax.ShapeDtypeStruct((keys, 2 * pairs * PAIR), BF16),
            jax.ShapeDtypeStruct((8, pairs * PAIR), F32),
        ],
        scratch_shapes=[pltpu.VMEM((tokens, keys), F32)],
        compiler_params=limit("attend_back"),
        cost_estimate=cost("attend_back"),
        name="attend_back",
    )(q, kv, grad, att, logs, own_doc, all_doc)


def row_mean(values):
    return jnp.mean(values, axis=-1, keepdims=True)


def column_sum(values):
    return jnp.sum(values.astype(F32), axis=0, keepdims=True)


def norm_back(grad_out, normed, inverse, scale_gain):
    grad_normed = grad_out * scale_gain
    inner = grad_normed - row_mean(grad_normed) - normed * row_mean(grad_normed * normed)
    return inner * inverse


def normalize(values):
    centred = values - row_mean(values)
    inverse = lax.rsqrt(row_mean(centred * centred) + EPSILON)
    return centred * inverse, inverse


def middle_kernel(grid, parts, att, hidden, cotangent, vec, b_expand, *refs):
    parts_b, parts_c, refs = refs[:parts], refs[parts : 2 * parts], refs[2 * parts :]
    result, first_out, normed_out, inverse_out, slope, second_out, low_out, keep, send, sums = refs[:10]
    wb, wc, active, staged, sem_b, sem_c, sem_out = refs[10:]
    width, wide = wb.shape[0], wc.shape[0]
    every = range(2 * grid.quads)
    chunks = [slice(n * width, (n + 1) * width) for n in range(wide // width + 1)]
    for n, cols in enumerate(chunks):
        fetch(grid, parts_b, wb, sem_b.at[n], cols)
    fetch(grid, parts_c, wc, sem_c, chunks[0])
    fetched(parts_b, wb, sem_b.at[0], chunks[0], every)
    mixed = dot(att[...], wb[:, :width]) + vec[2:3, :]
    normed, inverse = normalize(hidden[...].astype(F32) + mixed)
    normed_out[...] = normed
    inverse_out[...] = jnp.broadcast_to(inverse, inverse_out.shape)
    first = normed * vec[3:4, :] + vec[4:5, :]
    first_out[...] = first.astype(BF16)
    for n in range(wide // width):
        cols = chunks[n]
        fetched(parts_b, wb, sem_b.at[n + 1], chunks[n + 1], every)
        into = dot(first_out[...], wb[:, chunks[n + 1]]) + b_expand[:, cols]
        chance = 0.5 * (1.0 + lax.erf(into * (0.5**0.5)))
        density = jnp.exp(-0.5 * into * into) * ((2.0 * math.pi) ** -0.5)
        active[:, cols] = (into * chance).astype(BF16)
        slope[:, cols] = (chance + into * density).astype(BF16)
    fetched(parts_c, wc, sem_c, chunks[0], every)
    contracted = dot(active[...], wc[...]) + vec[5:6, :]
    normed, inverse = normalize(first + contracted)
    result[...] = (normed * vec[6:7, :] + vec[7:8, :]).astype(BF16)
    grad = cotangent[...].astype(F32)
    second = norm_back(grad, normed, inverse, vec[6:7, :])
    second_out[...] = second
    low = second.astype(BF16)
    low_out[...] = low
    sums[...] = jnp.zeros_like(sums)
    sums[5:6, :] = column_sum(low)
    sums[6:7, :] = column_sum(grad * normed)
    sums[7:8, :] = column_sum(grad)
    blocks = width // keep.shape[1]
    for n in range(wide // width):
        staged[chunks[n], :] = outer_sum(active[:, chunks[n]], low).astype(BF16)
        store_blocks(grid, staged, n * blocks, blocks, chunks[0], keep, send, sem_out)
    stored(grid, staged, every, chunks[0], keep, sem_out)


def middle(grid, att, hidden, cotangent, vec, b_expand, parts_b, parts_c):
    tokens, width = hidden.shape
    wide = b_expand.shape[1]
    blocks = jax.ShapeDtypeStruct((grid.quads,) + parts_c[0].shape[1:], BF16)
    return pl.pallas_call(
        functools.partial(middle_kernel, grid, len(parts_b)),
        in_specs=[VMEM] * 5 + [ANY] * (2 * len(parts_b)),
        out_specs=[VMEM] * 7 + [ANY] * 2 + [VMEM],
        out_shape=[
            jax.ShapeDtypeStruct((tokens, width), BF16),
            jax.ShapeDtypeStruct((tokens, width), BF16),
            jax.ShapeDtypeStruct((tokens, width), F32),
            jax.ShapeDtypeStruct((tokens, 128), F32),
            jax.ShapeDtypeStruct((tokens, wide), BF16),
            jax.ShapeDtypeStruct((tokens, width), F32),
            jax.ShapeDtypeStruct((tokens, width), BF16),
            blocks,
            blocks,
            jax.ShapeDtypeStruct((8, width), F32),
        ],
        scratch_shapes=[
            pltpu.VMEM((width, width + wide), BF16),
            pltpu.VMEM((wide, width), BF16),
            pltpu.VMEM((tokens, wide), BF16),
            pltpu.VMEM((wide, width), BF16),
            pltpu.SemaphoreType.DMA((wide // width + 1, 2 * grid.quads)),
            pltpu.SemaphoreType.DMA((2 * grid.quads,)),
            pltpu.SemaphoreType.DMA((2 * grid.quads,)),
        ],
        compiler_params=limit("middle"),
        cost_estimate=cost("middle"),
        name="middle",
    )(att, hidden, cotangent, vec, b_expand, *parts_b, *parts_c)


def dense_back_kernel(grid, parts, att, first, normed, inverse, slope, second, low, vec, *refs):
    parts_b, parts_c, refs = refs[:parts], refs[parts : 2 * parts], refs[2 * parts :]
    grad_sum, att_back, keep, send, sums, bias_sum = refs[:6]
    wb, wc, back, staged, sem_b, sem_c, sem_out = refs[6:]
    width, wide = wb.shape[0], wc.shape[0]
    every = range(2 * grid.quads)
    chunks = [slice(n * width, (n + 1) * width) for n in range(wide // width + 1)]
    per_chunk = len(every) * width // wide
    fetch(grid, parts_c, wc, sem_c, chunks[0])
    fetch(grid, parts_b, wb, sem_b, slice(0, wb.shape[1]))
    for n in range(wide // width):
        cols = chunks[n]
        fetched(parts_c, wc, sem_c, chunks[0], range(n * per_chunk, (n + 1) * per_chunk))
        piece = (times_transposed(low[...], wc[cols, :]) * slope[:, cols].astype(F32)).astype(BF16)
        back[:, cols] = piece
        bias_sum[:, cols] = column_sum(piece)
    fetched(parts_b, wb, sem_b, slice(0, wb.shape[1]), every)
    grad_first = second[...] + times_transposed(back[...], wb[:, width:])
    grad = norm_back(grad_first, normed[...], inverse[:, 0:1], vec[3:4, :])
    grad_sum[...] = grad
    mixed = grad.astype(BF16)
    att_back[...] = times_transposed(mixed, wb[:, :width]).astype(BF16)
    sums[...] = jnp.zeros_like(sums)
    sums[2:3, :] = column_sum(mixed)
    sums[3:4, :] = column_sum(grad_first * normed[...])
    sums[4:5, :] = column_sum(grad_first)
    for n, cols in enumerate(chunks):
        if n == 0:
            staged[:, cols] = outer_sum(att[...], mixed).astype(BF16)
        else:
            staged[:, cols] = outer_sum(first[...], back[:, chunks[n - 1]]).astype(BF16)
        store_blocks(grid, staged, 0, len(every), cols, keep, send, sem_out.at[n])
    for n, cols in enumerate(chunks):
        stored(grid, staged, every, cols, keep, sem_out.at[n])


def dense_back(grid, att, first, normed, inverse, slope, second, low, vec, parts_b, parts_c):
    tokens, width = att.shape
    wide = slope.shape[1]
    blocks = jax.ShapeDtypeStruct((grid.quads,) + parts_b[0].shape[1:], BF16)
    return pl.pallas_call(
        functools.partial(dense_back_kernel, grid, len(parts_b)),
        in_specs=[VMEM] * 8 + [ANY] * (2 * len(parts_b)),
        out_specs=[VMEM] * 2 + [ANY] * 2 + [VMEM] * 2,
        out_shape=[
            jax.ShapeDtypeStruct((tokens, width), F32),
            jax.ShapeDtypeStruct((tokens, width), BF16),
            blocks,
            blocks,
            jax.ShapeDtypeStruct((8, width), F32),
            jax.ShapeDtypeStruct((1, wide), F32),
        ],
        scratch_shapes=[
            pltpu.VMEM((width, width + wide), BF16),
            pltpu.VMEM((wide, width), BF16),
            pltpu.VMEM((tokens, wide), BF16),
            pltpu.VMEM((width, width + wide), BF16),
            pltpu.SemaphoreType.DMA((2 * grid.quads,)),
            pltpu.SemaphoreType.DMA((2 * grid.quads,)),
            pltpu.SemaphoreType.DMA((wide // width + 1, 2 * grid.quads)),
        ],
        compiler_params=limit("dense_back"),
        cost_estimate=cost("dense_back"),
        name="dense_back",
    )(att, first, normed, inverse, slope, second, low, vec, *parts_b, *parts_c)


def input_back_kernel(grid, parts, grad_sum, dq0, dq1, dkv0, dkv1, *refs):
    part_refs, outs = refs[:parts], refs[parts:-3]
    weights, total, sems = refs[-3:]
    tokens = grad_sum.shape[0]
    width = weights.shape[0]
    half = dkv0.shape[1]
    cols = slice(0, weights.shape[1])
    every = range(2 * grid.quads)
    fetch(grid, part_refs, weights, sems, cols)
    fetched(part_refs, weights, sems, cols, every)
    step = 256
    for n in range(width // step):
        to = slice(n * step, (n + 1) * step)
        total[...] = times_transposed(dkv0[...], weights[to, width : width + half]) + times_transposed(
            dkv1[...], weights[to, width + half : 3 * width]
        )
        for piece in range(len(outs)):
            back = total[piece * tokens : (piece + 1) * tokens, :]
            if piece == 0:
                back = back + times_transposed(dq0[...], weights[to, : half // 2])
                back = back + times_transposed(dq1[...], weights[to, half // 2 : width])
                back = back + grad_sum[:, to]
            outs[piece][:, to] = back.astype(outs[piece].dtype)


def input_back(grid, grad_sum, first_part, last_part, parts):
    tokens, width = grad_sum.shape
    return pl.pallas_call(
        functools.partial(input_back_kernel, grid, len(parts)),
        in_specs=[VMEM] * 5 + [ANY] * len(parts),
        out_specs=[VMEM] * grid.bands,
        out_shape=[jax.ShapeDtypeStruct((tokens, width), F32)]
        + [jax.ShapeDtypeStruct((tokens, width), BF16)] * (grid.bands - 1),
        scratch_shapes=[
            pltpu.VMEM((width, parts[0].shape[2]), BF16),
            pltpu.VMEM((grid.bands * tokens, 256), F32),
            pltpu.SemaphoreType.DMA((2 * grid.quads,)),
        ],
        compiler_params=limit("input_back"),
        cost_estimate=cost("input_back"),
        name="input_back",
    )(grad_sum, first_part[0], last_part[0], first_part[1], last_part[1], *parts)


def weight_back_kernel(grid, pieces, *refs):
    hidden, refs = refs[:pieces], refs[pieces:]
    dq0, dq1, dkv0, dkv1, sum0, sum1, sum2, sum3, bias_sum, keep, send = refs[:11]
    every, staged, stage, slab, sem_in, sem_out = refs[11:]
    tokens, width = hidden[0].shape
    half = dkv0.shape[1]
    blocks = 2 * grid.quads
    copies = [
        pltpu.make_async_copy(hidden[n], every.at[pl.ds(n * tokens, tokens), :], sem_in.at[n])
        for n in range(pieces)
    ]
    for copy in copies:
        copy.start()
    for copy in copies:
        copy.wait()
    chunks = [slice(n * width, (n + 1) * width) for n in range(3)] + [slice(3 * width, 3 * width + SLAB)]
    for n, item in enumerate((dkv0, dkv1)):
        staged[:, chunks[1 + n]] = outer_sum(every[...], item[...]).astype(BF16)
        store_blocks(grid, staged, 0, blocks, chunks[1 + n], keep, send, sem_out.at[1 + n])
    for n, item in enumerate((dq0, dq1)):
        cols = slice(n * half // 2, (n + 1) * half // 2)
        staged[:, cols] = outer_sum(every[0:tokens, :], item[...]).astype(BF16)
    store_blocks(grid, staged, 0, blocks, chunks[0], keep, send, sem_out.at[0])
    stage[...] = jnp.zeros_like(stage)
    stage[0:8, :] = sum2[...] + sum3[...]
    for n, item in enumerate((sum0, sum1)):
        stage[0:2, n * half // 2 : (n + 1) * half // 2] = item[0:2, :]
    slab[:, :128] = jnp.transpose(stage[...])
    slab[:, 128:] = jnp.zeros((width, SLAB - 128), F32)
    rows = width // grid.devices
    count = bias_sum.shape[1] // grid.devices
    for n in range(grid.devices):
        slab[n * rows : n * rows + 1, 16 : 16 + count] = bias_sum[:, n * count : (n + 1) * count]
    staged[:, chunks[3]] = slab[...].astype(BF16)
    store_blocks(grid, staged, 0, blocks, chunks[3], keep, send, sem_out.at[3])
    for n, cols in enumerate(chunks):
        stored(grid, staged, range(blocks), cols, keep, sem_out.at[n])


def weight_back(grid, hidden, first_part, last_part, sums, bias_sum):
    pieces = len(hidden)
    tokens, width = hidden[0].shape
    tall = width // (2 * grid.quads)
    blocks = jax.ShapeDtypeStruct((grid.quads, tall, 3 * width + SLAB), BF16)
    return pl.pallas_call(
        functools.partial(weight_back_kernel, grid, pieces),
        in_specs=[ANY] * pieces + [VMEM] * 9,
        out_specs=[ANY] * 2,
        out_shape=[blocks, blocks],
        scratch_shapes=[
            pltpu.VMEM((pieces * tokens, width), BF16),
            pltpu.VMEM((width, 3 * width + SLAB), BF16),
            pltpu.VMEM((128, width), F32),
            pltpu.VMEM((width, SLAB), F32),
            pltpu.SemaphoreType.DMA((pieces,)),
            pltpu.SemaphoreType.DMA((4, 2 * grid.quads)),
        ],
        compiler_params=limit("weight_back"),
        cost_estimate=cost("weight_back"),
        name="weight_back",
    )(
        *hidden,
        first_part[0],
        last_part[0],
        first_part[1],
        last_part[1],
        first_part[2],
        last_part[2],
        *sums,
        bias_sum,
    )


def add_kernel(left, right, later, out):
    out[...] = (left[...].astype(F32) + right[...].astype(F32)).astype(out.dtype)


def add_rows(left, right, later):
    return pl.pallas_call(
        add_kernel,
        in_specs=[VMEM, VMEM, ANY],
        out_specs=VMEM,
        out_shape=jax.ShapeDtypeStruct(left.shape, left.dtype),
        cost_estimate=cost("add_rows"),
        name="add_rows",
    )(left, right, later)


def unpack_kernel(parts, *refs):
    own, got, outs = refs[0], refs[1 : 1 + parts], refs[1 + parts : -2]
    total, stage = refs[-2:]
    rows, width = outs[0].shape
    result = own[...]
    for item in got:
        result = result + item[...].astype(F32)
    total[...] = result
    outs[0][...] = total[:, :width]
    for pair in range(width // PAIR):
        cols = slice(pair * PAIR, (pair + 1) * PAIR)
        for which in range(2):
            at = width + (2 * pair + which) * PAIR
            outs[1 + which][:, cols] = total[:, at : at + PAIR]
    stage[...] = jnp.zeros_like(stage)
    stage[0:rows, :] = total[:, 3 * width : 3 * width + 128]
    count = outs[-1].shape[0]
    outs[-1][...] = stage[0:1, 16 : 16 + count].reshape(count)
    stage[...] = jnp.transpose(stage[...])
    for n, out in enumerate(outs[3:-1]):
        out[...] = stage[n : n + 1, 0:rows].reshape(rows)


def unpack(own, got, width, count):
    rows = own.shape[0]
    matrix = jax.ShapeDtypeStruct((rows, width), F32)
    vector = jax.ShapeDtypeStruct((rows,), F32)
    return pl.pallas_call(
        functools.partial(unpack_kernel, len(got)),
        in_specs=[VMEM] * (1 + len(got)),
        out_specs=[VMEM] * 12,
        out_shape=[matrix] * 3 + [vector] * 8 + [jax.ShapeDtypeStruct((count,), F32)],
        scratch_shapes=[pltpu.VMEM(own.shape, F32), pltpu.VMEM((128, 128), F32)],
        cost_estimate=pl.CostEstimate(flops=10**9, bytes_accessed=1024, transcendentals=0),
        name="unpack",
    )(own, *got)


def per_device(
    grid,
    hidden_in,
    lengths,
    permutation,
    query_weight,
    query_bias,
    key_weight,
    value_weight,
    value_bias,
    mix_weight,
    mix_bias,
    first_gain,
    first_shift,
    expand_weight,
    expand_bias,
    contract_weight,
    contract_bias,
    second_gain,
    second_shift,
    cotangent,
):
    tokens, width = hidden_in.shape
    wide = contract_weight.shape[0] * grid.devices
    rows = query_weight.shape[0]
    bands = grid.bands

    vectors = [query_bias, value_bias, mix_bias, first_gain, first_shift, contract_bias, second_gain, second_shift]
    weights = [query_weight, key_weight, value_weight, mix_weight, expand_weight, contract_weight]
    shard_a, shard_b, shard_c, doc = pack(lengths, permutation, vectors, expand_bias, weights)

    pieces_a = z_direct(grid, shard_a)
    gather_a = Gather(grid, pieces_a)
    gather_a.near_step()
    pieces_b = z_direct(grid, after(shard_b, *pieces_a))
    pieces_c = z_direct(grid, after(shard_c, *pieces_a, gather_a.near_all))
    gather_b, gather_c = Gather(grid, pieces_b), Gather(grid, pieces_c)
    messages = [hidden_in]
    messages.append(grid.along_z(after(hidden_in, *pieces_b, *pieces_c, gather_a.near_all), 1))
    gather_a.far_step()
    gather_b.near_step()
    messages.append(grid.along_z(messages[1], 1))
    gather_c.near_step()
    parts_a = gather_a.core_step(messages[1])
    gather_b.far_step(messages[1], *gather_a.far_all)
    gather_c.far_step(messages[2])
    parts_b = gather_b.core_step(messages[2])
    for step in range(3, bands):
        messages.append(grid.along_z(messages[-1], 1))
    messages[0] = after(messages[0], gather_c.near_all, gather_b.near_all)

    docs_of = [doc] + [
        item[0:3, 3 * width + 128 :].astype(F32).reshape(1, 3 * 128)[:, :tokens] for item in pieces_a[1:]
    ]
    all_doc = jnp.concatenate(docs_of, axis=1)
    own_doc = doc.reshape(tokens, 1)
    q, kv, attended, logs, vec, b_expand = attend(grid, messages, parts_a, own_doc, all_doc, wide)
    gather_c.far_all = after(gather_c.far_all, attended)
    parts_c = gather_c.core_step()
    result, first, normed, inverse, slope, second, low, keep, send, sums_two = middle(
        grid, attended, hidden_in, cotangent, vec, b_expand, parts_b, parts_c
    )
    sum_c = Sum(grid, keep, send)
    grad_sum, attended_back, keep, send, sums_one, d_b_expand = dense_back(
        grid, attended, first, normed, inverse, slope, second, low, vec, parts_b, parts_c
    )
    sum_b = Sum(grid, keep, send)
    pairs = width // PAIR
    half = pairs // 2
    sum_c.core_step(grad_sum)
    attended_back = after(attended_back, sum_c.send)
    first_part = attend_back(0, half, q, kv, attended_back, attended, logs, own_doc, all_doc)
    sum_c.far_step(first_part)
    sum_b.core_step(sum_c.send)
    attended_back = after(attended_back, sum_b.send, sum_c.send)
    last_part = attend_back(half, pairs - half, q, kv, attended_back, attended, logs, own_doc, all_doc)
    sum_c.near_step(last_part)
    backs = input_back(grid, grad_sum, first_part, last_part, parts_a)
    sent = backs[bands - 1]
    sum_b.far_step(sent)
    d_contract = sum_c.z_step(sent)
    last_part = after(last_part, backs, sum_b.send, d_contract)
    keep, send = weight_back(grid, messages, first_part, last_part, (sums_two, sums_one), d_b_expand)
    sum_a = Sum(grid, keep, send)

    got = grid.along_z(sent, -1)
    sent = add_rows(backs[bands - 2], got, keep)
    sum_a.core_step(sent)
    sum_b.near_step(sum_a.send)
    for piece in range(bands - 2, 0, -1):
        got = grid.along_z(sent, -1)
        if piece == bands - 2:
            sum_a.far_step(sum_b.send)
        if piece > 1:
            sent = add_rows(backs[piece - 1], got, sum_a.send[0])
    sum_a.near_step(sent)
    d_b = sum_b.z_step(sum_a.send)
    grad_input = after(backs[0], d_b) + got.astype(F32)
    sum_a.move_z()
    d_query, d_key, d_value, *small, d_bias = unpack(sum_a.own, sum_a.got, width, expand_bias.shape[0])
    return (
        result,
        grad_input.astype(BF16),
        d_query,
        small[0],
        d_key,
        d_value,
        small[1],
        d_b[:, :width],
        small[2],
        small[3],
        small[4],
        d_b[:, width:],
        d_bias,
        d_contract,
        small[5],
        small[6],
        small[7],
    )


def solution(mesh):
    grid = Grid(mesh.shape["page"], mesh.shape["band"])
    matrix, vector = P(AXES, None), P(AXES)
    parameters = (
        matrix,
        vector,
        matrix,
        matrix,
        vector,
        matrix,
        vector,
        vector,
        vector,
        matrix,
        vector,
        matrix,
        vector,
        vector,
        vector,
    )
    return jax.shard_map(
        functools.partial(per_device, grid),
        mesh=mesh,
        in_specs=(matrix, P("page", None), P("page", "band")) + parameters + (matrix,),
        out_specs=(matrix, matrix) + parameters,
        check_vma=False,
    )
```

```python
import functools
import itertools
import math

import jax
import jax.numpy as jnp
from jax import lax
from jax.experimental import pallas as pl
from jax.experimental.pallas import tpu as pltpu
from jax.sharding import PartitionSpec as P

HEAD_DIM = 64
PAIR = 2 * HEAD_DIM
EPSILON = 1e-12
AXES = ("page", "band")
SLAB = 256
BF16, F32 = jnp.bfloat16, jnp.float32
COSTS = {
    "pack": 1,
    "attend": 1,
    "middle": 8,
    "dense_back": 10,
    "attend_back": 5,
    "input_back": 4,
    "weight_back": 5,
    "add_rows": 15,
}
LIMITS = {
    "pack": 60,
    "attend": 52,
    "middle": 36,
    "dense_back": 36,
    "attend_back": 54,
    "input_back": 32,
    "weight_back": 32,
    "add_rows": 60,
}


def limit(kernel):
    return pltpu.CompilerParams(vmem_limit_bytes=LIMITS[kernel] * 2**20)


def cost(kernel):
    return pl.CostEstimate(flops=int(COSTS[kernel] * 1.1e9), bytes_accessed=1024, transcendentals=0)


def dot(left, right):
    return lax.dot_general(left, right, (((1,), (0,)), ((), ())), preferred_element_type=F32)


def times_transposed(left, right):
    return lax.dot_general(left, right, (((1,), (1,)), ((), ())), preferred_element_type=F32)


def outer_sum(left, right):
    return lax.dot_general(left, right, (((0,), (0,)), ((), ())), preferred_element_type=F32)


class Grid:
    def __init__(self, pages, bands):
        self.side = math.isqrt(pages // 2)
        assert self.side * self.side * 2 == pages
        self.bands = bands
        self.devices = pages * bands
        self.quads = self.side * self.side

    def linear(self, i, j, c, z):
        return ((i * self.side + j) * 2 + c) * self.bands + z

    def permute(self, array, move):
        side, bands = self.side, self.bands
        pairs = []
        for i, j, c, z in itertools.product(range(side), range(side), range(2), range(bands)):
            ti, tj, tc, tz = move(i, j, c, z)
            pairs.append((self.linear(i, j, c, z), self.linear(ti % side, tj % side, tc, tz % bands)))
        return lax.ppermute(array, AXES, pairs)

    def along_z(self, array, step):
        return self.permute(array, lambda i, j, c, z: (i, j, c, z + step))

    def near(self, array, step):
        return self.permute(
            array, lambda i, j, c, z: (i, j + step, c, z) if c == 0 else (i + step, j, c, z)
        )

    def far(self, array, step):
        return self.permute(
            array, lambda i, j, c, z: (i + step, j, c, z) if c == 0 else (i, j + step, c, z)
        )

    def across(self, array):
        return self.permute(array, lambda i, j, c, z: (i, j, 1 - c, z))

    def place(self):
        page, z = lax.axis_index("page"), lax.axis_index("band")
        return page // (2 * self.side), (page // 2) % self.side, page % 2, z


def after(value, *others):
    return lax.optimization_barrier((value, others))[0]


def z_direct(grid, shard):
    return [shard] + [grid.along_z(shard, step) for step in range(1, grid.bands)]


class Gather:
    def __init__(self, grid, pieces):
        self.grid = grid
        rows, width = pieces[0].shape
        z = lax.axis_index("band")
        block = jnp.zeros((grid.bands, rows, width), pieces[0].dtype)
        for step, piece in enumerate(pieces):
            block = lax.dynamic_update_slice(block, piece[None], ((z - step) % grid.bands, 0, 0))
        self.block = block.reshape(grid.bands * rows, width)

    def near_step(self, *pins):
        block = after(self.block, *pins)
        got = [self.grid.near(block, step) for step in range(1, self.grid.side)]
        self.near_all = jnp.stack([self.block] + got)

    def far_step(self, *pins):
        near_all = after(self.near_all, *pins)
        self.far_all = [self.grid.far(near_all, step) for step in range(1, self.grid.side)]

    def core_step(self, *pins):
        parts = [self.near_all] + self.far_all
        first = self.grid.across(after(self.near_all, *pins))
        return parts + [first] + [self.grid.across(item) for item in self.far_all]


def fetch(grid, parts, whole, sems, cols):
    i, j, c, _ = grid.place()
    tall = parts[0].shape[1]
    for d in range(2):
        core = (c + d) % 2
        for a in range(grid.side):
            for b in range(grid.side):
                di = jnp.where(core == 0, a, b)
                dj = jnp.where(core == 0, b, a)
                up = (i - di + grid.side) % grid.side
                left = (j - dj + grid.side) % grid.side
                index = (up * grid.side + left) * 2 + core
                pltpu.make_async_copy(
                    parts[d * grid.side + a].at[b, :, cols],
                    whole.at[pl.ds(pl.multiple_of(index * tall, 8), tall), cols],
                    sems.at[index],
                ).start()


def fetched(parts, whole, sems, cols, blocks):
    tall = parts[0].shape[1]
    for n in blocks:
        pltpu.make_async_copy(
            parts[0].at[0, :, cols], whole.at[pl.ds(n * tall, tall), cols], sems.at[n]
        ).wait()


def store_blocks(grid, staged, first, blocks, cols, keep, send, sems):
    i, j, c, _ = grid.place()
    tall = keep.shape[1]
    for n in range(blocks):
        block = first + n
        core = block % 2
        ti, tj = block // (2 * grid.side), (block // 2) % grid.side
        di = (ti - i + grid.side) % grid.side
        dj = (tj - j + grid.side) % grid.side
        slot = di * grid.side + dj if core == 0 else dj * grid.side + di
        source = staged.at[pl.ds(block * tall, tall), cols]

        @pl.when(c == core)
        def _():
            pltpu.make_async_copy(source, keep.at[slot, :, cols], sems.at[block]).start()

        @pl.when(c != core)
        def _():
            pltpu.make_async_copy(source, send.at[slot, :, cols], sems.at[block]).start()


def stored(grid, staged, blocks, cols, keep, sems):
    tall = keep.shape[1]
    for block in blocks:
        source = staged.at[pl.ds(block * tall, tall), cols]
        pltpu.make_async_copy(source, keep.at[0, :, cols], sems.at[block]).wait()


class Sum:
    def __init__(self, grid, keep, send):
        self.grid, self.send = grid, send
        self.terms = [keep]

    def total(self, at):
        result = self.terms[0][at].astype(F32)
        for item in self.terms[1:]:
            result = result + item[at].astype(F32)
        return result

    def move_core(self):
        self.got = self.grid.across(self.send)

    def add_core(self, *pins):
        side = self.grid.side
        self.terms = after(self.terms, *pins) + [self.got]
        self.send = [self.total(slice(a * side, (a + 1) * side)).astype(BF16) for a in range(1, side)]

    def move_far(self):
        self.got = [self.grid.far(item, a) for a, item in enumerate(self.send, 1)]

    def add_far(self, *pins):
        self.terms = after(self.terms, *pins) + self.got
        self.send = [self.total(b).astype(BF16) for b in range(1, self.grid.side)]

    def move_near(self):
        self.got = [self.grid.near(item, b)[None] for b, item in enumerate(self.send, 1)]

    def add_near(self, *pins):
        bands = self.grid.bands
        self.terms = after(self.terms, *pins) + self.got
        own = self.total(0)
        own = own.reshape(bands, own.shape[0] // bands, own.shape[1])
        z = lax.axis_index("band")
        self.own = lax.dynamic_index_in_dim(own, z, 0, False)
        self.send = [
            lax.dynamic_index_in_dim(own, (z + step) % bands, 0, False).astype(BF16)
            for step in range(1, bands)
        ]

    def move_z(self):
        self.got = [self.grid.along_z(item, step) for step, item in enumerate(self.send, 1)]

    def add_z(self, *pins):
        own = after(self.own, *pins)
        for item in self.got:
            own = own + item.astype(F32)
        return own

    def core_step(self, *pins):
        self.move_core()
        self.add_core(*pins)

    def far_step(self, *pins):
        self.move_far()
        self.add_far(*pins)

    def near_step(self, *pins):
        self.move_near()
        self.add_near(*pins)

    def z_step(self, *pins):
        self.move_z()
        return self.add_z(*pins)


def pack_kernel(lengths, permutation, *refs):
    vectors, bias = refs[:8], refs[8]
    wq, wk, wv, wo, wi, wc = refs[9:15]
    a_out, b_out, c_out, doc_out = refs[15:19]
    stage, tall = refs[19:]
    rows, width = wq.shape
    docs = lengths.shape[1]
    tokens = permutation.shape[1]
    earlier = lax.broadcasted_iota(jnp.int32, (docs, docs), 1) <= lax.broadcasted_iota(
        jnp.int32, (docs, docs), 0
    )
    ends = jnp.sum(jnp.where(earlier, lengths[...], 0).astype(F32), axis=1, keepdims=True)
    marks = jnp.sum(
        jnp.where(permutation[...].astype(F32) >= ends, 1.0, 0.0), axis=0, keepdims=True
    )
    doc_out[...] = marks
    a_out[:, :width] = wq[...].astype(BF16)
    for pair in range(width // PAIR):
        at = width + 2 * pair * PAIR
        cols = slice(pair * PAIR, (pair + 1) * PAIR)
        a_out[:, at : at + PAIR] = wk[:, cols].astype(BF16)
        a_out[:, at + PAIR : at + 2 * PAIR] = wv[:, cols].astype(BF16)
    stage[...] = jnp.zeros_like(stage)
    for n, item in enumerate(vectors):
        stage[n : n + 1, 0:rows] = item[...].reshape(1, rows)
    tall[...] = jnp.transpose(stage[...])
    tall[0:1, 16 : 16 + bias.shape[0]] = bias[...].reshape(1, bias.shape[0])
    a_out[:, 3 * width : 3 * width + 128] = tall[0:rows, :].astype(BF16)
    tall[...] = jnp.zeros_like(tall)
    for n in range(3):
        count = min(128, tokens - n * 128)
        tall[n : n + 1, 0:count] = marks[:, n * 128 : n * 128 + count]
    a_out[:, 3 * width + 128 :] = tall[0:rows, :].astype(BF16)
    b_out[:, :width] = wo[...].astype(BF16)
    b_out[:, width:] = wi[...].astype(BF16)
    c_out[...] = wc[...].astype(BF16)


def pack(lengths, permutation, vectors, bias, weights):
    rows, width = weights[0].shape
    wide = weights[4].shape[1]
    tokens = permutation.shape[1]
    assert tokens <= 3 * 128 and bias.shape[0] <= 112 and rows <= 128
    vmem = pl.BlockSpec(memory_space=pltpu.VMEM)
    return pl.pallas_call(
        pack_kernel,
        in_specs=[vmem] * 17,
        out_specs=[vmem] * 4,
        out_shape=[
            jax.ShapeDtypeStruct((rows, 3 * width + SLAB), BF16),
            jax.ShapeDtypeStruct((rows, width + wide), BF16),
            jax.ShapeDtypeStruct(weights[5].shape, BF16),
            jax.ShapeDtypeStruct((1, tokens), F32),
        ],
        scratch_shapes=[pltpu.VMEM((128, 128), F32), pltpu.VMEM((128, 128), F32)],
        compiler_params=limit("pack"),
        cost_estimate=cost("pack"),
        name="pack",
    )(lengths, permutation, *vectors, bias, *weights)


def head_mask(rows, head):
    lanes = lax.broadcasted_iota(jnp.int32, (rows, PAIR), 1)
    return (lanes // HEAD_DIM) == head


def attend_kernel(grid, pieces, parts, *refs):
    hidden, refs = refs[:pieces], refs[pieces:]
    part_refs, refs = refs[:parts], refs[parts:]
    own_doc, all_doc = refs[:2]
    q_out, kv_out, att_out, log_out, vec_out, bias_out, bias, weights, slab, sems = refs[2:]
    tokens = q_out.shape[0]
    keys = kv_out.shape[0]
    width = weights.shape[0]
    step = q_out.shape[1]
    group = pl.program_id(0)

    groups = width // step
    every = range(2 * grid.quads)
    slab_cols = slice(3 * width, weights.shape[1])

    def columns(n):
        first = slice(n * step, (n + 1) * step)
        return first, slice(width + 2 * n * step, width + 2 * (n + 1) * step)

    @pl.when(group == 0)
    def _():
        fetch(grid, part_refs, weights, sems.at[0], slab_cols)
        for n in range(groups):
            for m, cols in enumerate(columns(n)):
                fetch(grid, part_refs, weights, sems.at[1 + 2 * n + m], cols)
        bias[...] = jnp.where(own_doc[...] == all_doc[...], 0.0, -1e30).astype(F32)
        fetched(part_refs, weights, sems.at[0], slab_cols, every)
        slab[...] = weights[:, 3 * width : 3 * width + 128].astype(F32)
        vec_out[...] = jnp.transpose(slab[...])[0:16, :]
        rows = width // grid.devices
        count = bias_out.shape[1] // grid.devices
        for n in range(grid.devices):
            bias_out[:, n * count : (n + 1) * count] = slab[n * rows : n * rows + 1, 16 : 16 + count]

    for n in range(groups):

        @pl.when(group == n)
        def _():
            for m, cols in enumerate(columns(n)):
                fetched(part_refs, weights, sems.at[1 + 2 * n + m], cols, every)

    at = pl.multiple_of(group * step, step)
    query_bias = vec_out[0:1, pl.ds(at, step)]
    value_bias = vec_out[1:2, pl.ds(at, step)]
    q_out[...] = (dot(hidden[0][...], weights[:, pl.ds(at, step)]) + query_bias).astype(BF16)
    pairs = step // PAIR
    for p in range(pieces):
        rows = slice(p * tokens, (p + 1) * tokens)
        for pair in range(pairs):
            there = pl.multiple_of(width + 2 * at + 2 * pair * PAIR, 2 * PAIR)
            both = dot(hidden[p][...], weights[:, pl.ds(there, 2 * PAIR)])
            to = 2 * pair * PAIR
            kv_out[rows, to : to + PAIR] = both[:, :PAIR].astype(BF16)
            value = both[:, PAIR:] + value_bias[:, pair * PAIR : (pair + 1) * PAIR]
            kv_out[rows, to + PAIR : to + 2 * PAIR] = value.astype(BF16)
    lane = lax.broadcasted_iota(jnp.int32, (tokens, 128), 1)
    logs = jnp.zeros((tokens, 128), F32)
    ones = jnp.ones((keys, PAIR), BF16)
    for pair in range(pairs):
        cols = slice(pair * PAIR, (pair + 1) * PAIR)
        query = q_out[:, cols]
        key = kv_out[:, 2 * pair * PAIR : (2 * pair + 1) * PAIR]
        value = jnp.concatenate([kv_out[:, (2 * pair + 1) * PAIR : (2 * pair + 2) * PAIR], ones], axis=1)
        outs = []
        for head in range(2):
            picked = jnp.where(head_mask(tokens, head), query * HEAD_DIM**-0.5, 0).astype(BF16)
            scores = times_transposed(picked, key) + bias[...]
            peak = jnp.max(scores, axis=1, keepdims=True)
            weights = jnp.exp(scores - peak).astype(BF16)
            both = dot(weights, value)
            outs.append(both[:, :PAIR] / both[:, PAIR:])
            total = peak + jnp.log(both[:, PAIR:])
            logs = jnp.where(lane == pair * 2 + head, total, logs)
        att_out[:, cols] = jnp.where(head_mask(tokens, 0), outs[0], outs[1]).astype(BF16)
    log_out[...] = logs[None]


ANY = pl.BlockSpec(memory_space=pl.ANY)
VMEM = pl.BlockSpec(memory_space=pltpu.VMEM)


def attend(grid, hidden, parts, own_doc, all_doc, wide):
    pieces = len(hidden)
    tokens, width = hidden[0].shape
    keys = pieces * tokens
    step = 256
    groups = width // step
    whole = lambda shape: pl.BlockSpec(shape, lambda g: (0, 0))
    tall = lambda rows: pl.BlockSpec((rows, step), lambda g: (0, g))
    return pl.pallas_call(
        functools.partial(attend_kernel, grid, pieces, len(parts)),
        grid=(groups,),
        in_specs=[whole(item.shape) for item in hidden]
        + [ANY] * len(parts)
        + [whole(own_doc.shape), whole(all_doc.shape)],
        out_specs=[
            tall(tokens),
            pl.BlockSpec((keys, 2 * step), lambda g: (0, g)),
            tall(tokens),
            pl.BlockSpec((1, tokens, 128), lambda g: (g, 0, 0)),
            whole((16, width)),
            whole((1, wide)),
        ],
        out_shape=[
            jax.ShapeDtypeStruct((tokens, width), BF16),
            jax.ShapeDtypeStruct((keys, 2 * width), BF16),
            jax.ShapeDtypeStruct((tokens, width), BF16),
            jax.ShapeDtypeStruct((groups, tokens, 128), F32),
            jax.ShapeDtypeStruct((16, width), F32),
            jax.ShapeDtypeStruct((1, wide), F32),
        ],
        scratch_shapes=[
            pltpu.VMEM((tokens, keys), F32),
            pltpu.VMEM((width, parts[0].shape[2]), BF16),
            pltpu.VMEM((width, 128), F32),
            pltpu.SemaphoreType.DMA((1 + 2 * groups, 2 * grid.quads)),
        ],
        compiler_params=limit("attend"),
        cost_estimate=cost("attend"),
        name="attend",
    )(*hidden, *parts, own_doc, all_doc)


def attend_back_kernel(start, q, kv, grad, att, logs, own_doc, doc, dq_out, dkv_out, sum_out, bias):
    tokens = q.shape[0]
    pair = pl.program_id(0) + start

    @pl.when(pair == start)
    def _():
        bias[...] = jnp.where(own_doc[...] == doc[...], 0.0, -1e30).astype(F32)

    lane = lax.broadcasted_iota(jnp.int32, (tokens, 128), 1)
    key, value = kv[:, :PAIR], kv[:, PAIR:]
    product = grad[...].astype(F32) * att[...].astype(F32)
    dq, dk, dv = [], 0.0, 0.0
    for head in range(2):
        mask = head_mask(tokens, head)
        query = jnp.where(mask, q[...] * HEAD_DIM**-0.5, 0).astype(BF16)
        part = jnp.where(mask, grad[...], 0).astype(BF16)
        slot = (pair % 2) * 2 + head
        log_total = jnp.sum(jnp.where(lane == slot, logs[0], 0.0), axis=1, keepdims=True)
        inner = jnp.sum(jnp.where(mask, product, 0.0), axis=1, keepdims=True)
        weights = jnp.exp(times_transposed(query, key) + bias[...] - log_total)
        back = (weights * (times_transposed(part, value) - inner)).astype(BF16)
        dq.append(dot(back, key) * HEAD_DIM**-0.5)
        dk = dk + outer_sum(back, query)
        dv = dv + outer_sum(weights.astype(BF16), part)
    dq_low = jnp.where(head_mask(tokens, 0), dq[0], dq[1]).astype(BF16)
    dq_out[...] = dq_low
    dkv_out[:, :PAIR] = dk.astype(BF16)
    dv_low = dv.astype(BF16)
    dkv_out[:, PAIR:] = dv_low
    sum_out[0:1, :] = column_sum(dq_low)
    sum_out[1:2, :] = column_sum(dv_low)


def attend_back(start, pairs, q, kv, grad, att, logs, own_doc, all_doc):
    tokens = q.shape[0]
    keys = kv.shape[0]
    short = pl.BlockSpec((tokens, PAIR), lambda g: (0, start + g))
    whole = lambda shape: pl.BlockSpec(shape, lambda g: (0, 0))
    return pl.pallas_call(
        functools.partial(attend_back_kernel, start),
        grid=(pairs,),
        in_specs=[
            short,
            pl.BlockSpec((keys, 2 * PAIR), lambda g: (0, start + g)),
            short,
            short,
            pl.BlockSpec((1, tokens, 128), lambda g: ((start + g) // 2, 0, 0)),
            whole(own_doc.shape),
            whole(all_doc.shape),
        ],
        out_specs=[
            pl.BlockSpec((tokens, PAIR), lambda g: (0, g)),
            pl.BlockSpec((keys, 2 * PAIR), lambda g: (0, g)),
            pl.BlockSpec((8, PAIR), lambda g: (0, g)),
        ],
        out_shape=[
            jax.ShapeDtypeStruct((tokens, pairs * PAIR), BF16),
            jax.ShapeDtypeStruct((keys, 2 * pairs * PAIR), BF16),
            jax.ShapeDtypeStruct((8, pairs * PAIR), F32),
        ],
        scratch_shapes=[pltpu.VMEM((tokens, keys), F32)],
        compiler_params=limit("attend_back"),
        cost_estimate=cost("attend_back"),
        name="attend_back",
    )(q, kv, grad, att, logs, own_doc, all_doc)


def row_mean(values):
    return jnp.mean(values, axis=-1, keepdims=True)


def column_sum(values):
    return jnp.sum(values.astype(F32), axis=0, keepdims=True)


def norm_back(grad_out, normed, inverse, scale_gain):
    grad_normed = grad_out * scale_gain
    inner = grad_normed - row_mean(grad_normed) - normed * row_mean(grad_normed * normed)
    return inner * inverse


def normalize(values):
    centred = values - row_mean(values)
    inverse = lax.rsqrt(row_mean(centred * centred) + EPSILON)
    return centred * inverse, inverse


def middle_kernel(grid, parts, att, hidden, cotangent, vec, b_expand, *refs):
    parts_b, parts_c, refs = refs[:parts], refs[parts : 2 * parts], refs[2 * parts :]
    result, first_out, normed_out, inverse_out, slope, second_out, low_out, keep, send, sums = refs[:10]
    wb, wc, active, staged, sem_b, sem_c, sem_out = refs[10:]
    width, wide = wb.shape[0], wc.shape[0]
    every = range(2 * grid.quads)
    chunks = [slice(n * width, (n + 1) * width) for n in range(wide // width + 1)]
    for n, cols in enumerate(chunks):
        fetch(grid, parts_b, wb, sem_b.at[n], cols)
    fetch(grid, parts_c, wc, sem_c, chunks[0])
    fetched(parts_b, wb, sem_b.at[0], chunks[0], every)
    mixed = dot(att[...], wb[:, :width]) + vec[2:3, :]
    normed, inverse = normalize(hidden[...].astype(F32) + mixed)
    normed_out[...] = normed
    inverse_out[...] = jnp.broadcast_to(inverse, inverse_out.shape)
    first = normed * vec[3:4, :] + vec[4:5, :]
    first_out[...] = first.astype(BF16)
    for n in range(wide // width):
        cols = chunks[n]
        fetched(parts_b, wb, sem_b.at[n + 1], chunks[n + 1], every)
        into = dot(first_out[...], wb[:, chunks[n + 1]]) + b_expand[:, cols]
        chance = 0.5 * (1.0 + lax.erf(into * (0.5**0.5)))
        density = jnp.exp(-0.5 * into * into) * ((2.0 * math.pi) ** -0.5)
        active[:, cols] = (into * chance).astype(BF16)
        slope[:, cols] = (chance + into * density).astype(BF16)
    fetched(parts_c, wc, sem_c, chunks[0], every)
    contracted = dot(active[...], wc[...]) + vec[5:6, :]
    normed, inverse = normalize(first + contracted)
    result[...] = (normed * vec[6:7, :] + vec[7:8, :]).astype(BF16)
    grad = cotangent[...].astype(F32)
    second = norm_back(grad, normed, inverse, vec[6:7, :])
    second_out[...] = second
    low = second.astype(BF16)
    low_out[...] = low
    sums[...] = jnp.zeros_like(sums)
    sums[5:6, :] = column_sum(low)
    sums[6:7, :] = column_sum(grad * normed)
    sums[7:8, :] = column_sum(grad)
    blocks = width // keep.shape[1]
    for n in range(wide // width):
        staged[chunks[n], :] = outer_sum(active[:, chunks[n]], low).astype(BF16)
        store_blocks(grid, staged, n * blocks, blocks, chunks[0], keep, send, sem_out)
    stored(grid, staged, every, chunks[0], keep, sem_out)


def middle(grid, att, hidden, cotangent, vec, b_expand, parts_b, parts_c):
    tokens, width = hidden.shape
    wide = b_expand.shape[1]
    blocks = jax.ShapeDtypeStruct((grid.quads,) + parts_c[0].shape[1:], BF16)
    return pl.pallas_call(
        functools.partial(middle_kernel, grid, len(parts_b)),
        in_specs=[VMEM] * 5 + [ANY] * (2 * len(parts_b)),
        out_specs=[VMEM] * 7 + [ANY] * 2 + [VMEM],
        out_shape=[
            jax.ShapeDtypeStruct((tokens, width), BF16),
            jax.ShapeDtypeStruct((tokens, width), BF16),
            jax.ShapeDtypeStruct((tokens, width), F32),
            jax.ShapeDtypeStruct((tokens, 128), F32),
            jax.ShapeDtypeStruct((tokens, wide), BF16),
            jax.ShapeDtypeStruct((tokens, width), F32),
            jax.ShapeDtypeStruct((tokens, width), BF16),
            blocks,
            blocks,
            jax.ShapeDtypeStruct((8, width), F32),
        ],
        scratch_shapes=[
            pltpu.VMEM((width, width + wide), BF16),
            pltpu.VMEM((wide, width), BF16),
            pltpu.VMEM((tokens, wide), BF16),
            pltpu.VMEM((wide, width), BF16),
            pltpu.SemaphoreType.DMA((wide // width + 1, 2 * grid.quads)),
            pltpu.SemaphoreType.DMA((2 * grid.quads,)),
            pltpu.SemaphoreType.DMA((2 * grid.quads,)),
        ],
        compiler_params=limit("middle"),
        cost_estimate=cost("middle"),
        name="middle",
    )(att, hidden, cotangent, vec, b_expand, *parts_b, *parts_c)


def dense_back_kernel(grid, parts, att, first, normed, inverse, slope, second, low, vec, *refs):
    parts_b, parts_c, refs = refs[:parts], refs[parts : 2 * parts], refs[2 * parts :]
    grad_sum, att_back, keep, send, sums, bias_sum = refs[:6]
    wb, wc, back, staged, sem_b, sem_c, sem_out = refs[6:]
    width, wide = wb.shape[0], wc.shape[0]
    every = range(2 * grid.quads)
    chunks = [slice(n * width, (n + 1) * width) for n in range(wide // width + 1)]
    per_chunk = len(every) * width // wide
    fetch(grid, parts_c, wc, sem_c, chunks[0])
    fetch(grid, parts_b, wb, sem_b, slice(0, wb.shape[1]))
    for n in range(wide // width):
        cols = chunks[n]
        fetched(parts_c, wc, sem_c, chunks[0], range(n * per_chunk, (n + 1) * per_chunk))
        piece = (times_transposed(low[...], wc[cols, :]) * slope[:, cols].astype(F32)).astype(BF16)
        back[:, cols] = piece
        bias_sum[:, cols] = column_sum(piece)
    fetched(parts_b, wb, sem_b, slice(0, wb.shape[1]), every)
    grad_first = second[...] + times_transposed(back[...], wb[:, width:])
    grad = norm_back(grad_first, normed[...], inverse[:, 0:1], vec[3:4, :])
    grad_sum[...] = grad
    mixed = grad.astype(BF16)
    att_back[...] = times_transposed(mixed, wb[:, :width]).astype(BF16)
    sums[...] = jnp.zeros_like(sums)
    sums[2:3, :] = column_sum(mixed)
    sums[3:4, :] = column_sum(grad_first * normed[...])
    sums[4:5, :] = column_sum(grad_first)
    for n, cols in enumerate(chunks):
        if n == 0:
            staged[:, cols] = outer_sum(att[...], mixed).astype(BF16)
        else:
            staged[:, cols] = outer_sum(first[...], back[:, chunks[n - 1]]).astype(BF16)
        store_blocks(grid, staged, 0, len(every), cols, keep, send, sem_out.at[n])
    for n, cols in enumerate(chunks):
        stored(grid, staged, every, cols, keep, sem_out.at[n])


def dense_back(grid, att, first, normed, inverse, slope, second, low, vec, parts_b, parts_c):
    tokens, width = att.shape
    wide = slope.shape[1]
    blocks = jax.ShapeDtypeStruct((grid.quads,) + parts_b[0].shape[1:], BF16)
    return pl.pallas_call(
        functools.partial(dense_back_kernel, grid, len(parts_b)),
        in_specs=[VMEM] * 8 + [ANY] * (2 * len(parts_b)),
        out_specs=[VMEM] * 2 + [ANY] * 2 + [VMEM] * 2,
        out_shape=[
            jax.ShapeDtypeStruct((tokens, width), F32),
            jax.ShapeDtypeStruct((tokens, width), BF16),
            blocks,
            blocks,
            jax.ShapeDtypeStruct((8, width), F32),
            jax.ShapeDtypeStruct((1, wide), F32),
        ],
        scratch_shapes=[
            pltpu.VMEM((width, width + wide), BF16),
            pltpu.VMEM((wide, width), BF16),
            pltpu.VMEM((tokens, wide), BF16),
            pltpu.VMEM((width, width + wide), BF16),
            pltpu.SemaphoreType.DMA((2 * grid.quads,)),
            pltpu.SemaphoreType.DMA((2 * grid.quads,)),
            pltpu.SemaphoreType.DMA((wide // width + 1, 2 * grid.quads)),
        ],
        compiler_params=limit("dense_back"),
        cost_estimate=cost("dense_back"),
        name="dense_back",
    )(att, first, normed, inverse, slope, second, low, vec, *parts_b, *parts_c)


def input_back_kernel(grid, parts, grad_sum, dq0, dq1, dkv0, dkv1, *refs):
    part_refs, outs = refs[:parts], refs[parts:-3]
    weights, total, sems = refs[-3:]
    tokens = grad_sum.shape[0]
    width = weights.shape[0]
    half = dkv0.shape[1]
    cols = slice(0, weights.shape[1])
    every = range(2 * grid.quads)
    fetch(grid, part_refs, weights, sems, cols)
    fetched(part_refs, weights, sems, cols, every)
    step = 256
    for n in range(width // step):
        to = slice(n * step, (n + 1) * step)
        total[...] = times_transposed(dkv0[...], weights[to, width : width + half]) + times_transposed(
            dkv1[...], weights[to, width + half : 3 * width]
        )
        for piece in range(len(outs)):
            back = total[piece * tokens : (piece + 1) * tokens, :]
            if piece == 0:
                back = back + times_transposed(dq0[...], weights[to, : half // 2])
                back = back + times_transposed(dq1[...], weights[to, half // 2 : width])
                back = back + grad_sum[:, to]
            outs[piece][:, to] = back.astype(outs[piece].dtype)


def input_back(grid, grad_sum, first_part, last_part, parts):
    tokens, width = grad_sum.shape
    return pl.pallas_call(
        functools.partial(input_back_kernel, grid, len(parts)),
        in_specs=[VMEM] * 5 + [ANY] * len(parts),
        out_specs=[VMEM] * grid.bands,
        out_shape=[jax.ShapeDtypeStruct((tokens, width), F32)]
        + [jax.ShapeDtypeStruct((tokens, width), BF16)] * (grid.bands - 1),
        scratch_shapes=[
            pltpu.VMEM((width, parts[0].shape[2]), BF16),
            pltpu.VMEM((grid.bands * tokens, 256), F32),
            pltpu.SemaphoreType.DMA((2 * grid.quads,)),
        ],
        compiler_params=limit("input_back"),
        cost_estimate=cost("input_back"),
        name="input_back",
    )(grad_sum, first_part[0], last_part[0], first_part[1], last_part[1], *parts)


def weight_back_kernel(grid, pieces, *refs):
    hidden, refs = refs[:pieces], refs[pieces:]
    dq0, dq1, dkv0, dkv1, sum0, sum1, sum2, sum3, bias_sum, keep, send = refs[:11]
    every, staged, stage, slab, sem_in, sem_out = refs[11:]
    tokens, width = hidden[0].shape
    half = dkv0.shape[1]
    blocks = 2 * grid.quads
    copies = [
        pltpu.make_async_copy(hidden[n], every.at[pl.ds(n * tokens, tokens), :], sem_in.at[n])
        for n in range(pieces)
    ]
    for copy in copies:
        copy.start()
    chunks = [slice(n * width, (n + 1) * width) for n in range(3)] + [slice(3 * width, 3 * width + SLAB)]
    copies[0].wait()
    for n, item in enumerate((dq0, dq1)):
        cols = slice(n * half // 2, (n + 1) * half // 2)
        staged[:, cols] = outer_sum(every[0:tokens, :], item[...]).astype(BF16)
    store_blocks(grid, staged, 0, blocks, chunks[0], keep, send, sem_out.at[0])
    for copy in copies[1:]:
        copy.wait()
    for n, item in enumerate((dkv0, dkv1)):
        staged[:, chunks[1 + n]] = outer_sum(every[...], item[...]).astype(BF16)
        store_blocks(grid, staged, 0, blocks, chunks[1 + n], keep, send, sem_out.at[1 + n])
    stage[...] = jnp.zeros_like(stage)
    stage[0:8, :] = sum2[...] + sum3[...]
    for n, item in enumerate((sum0, sum1)):
        stage[0:2, n * half // 2 : (n + 1) * half // 2] = item[0:2, :]
    slab[:, :128] = jnp.transpose(stage[...])
    slab[:, 128:] = jnp.zeros((width, SLAB - 128), F32)
    rows = width // grid.devices
    count = bias_sum.shape[1] // grid.devices
    for n in range(grid.devices):
        slab[n * rows : n * rows + 1, 16 : 16 + count] = bias_sum[:, n * count : (n + 1) * count]
    staged[:, chunks[3]] = slab[...].astype(BF16)
    store_blocks(grid, staged, 0, blocks, chunks[3], keep, send, sem_out.at[3])
    for n, cols in enumerate(chunks):
        stored(grid, staged, range(blocks), cols, keep, sem_out.at[n])


def weight_back(grid, hidden, first_part, last_part, sums, bias_sum):
    pieces = len(hidden)
    tokens, width = hidden[0].shape
    tall = width // (2 * grid.quads)
    blocks = jax.ShapeDtypeStruct((grid.quads, tall, 3 * width + SLAB), BF16)
    return pl.pallas_call(
        functools.partial(weight_back_kernel, grid, pieces),
        in_specs=[ANY] * pieces + [VMEM] * 9,
        out_specs=[ANY] * 2,
        out_shape=[blocks, blocks],
        scratch_shapes=[
            pltpu.VMEM((pieces * tokens, width), BF16),
            pltpu.VMEM((width, 3 * width + SLAB), BF16),
            pltpu.VMEM((128, width), F32),
            pltpu.VMEM((width, SLAB), F32),
            pltpu.SemaphoreType.DMA((pieces,)),
            pltpu.SemaphoreType.DMA((4, 2 * grid.quads)),
        ],
        compiler_params=limit("weight_back"),
        cost_estimate=cost("weight_back"),
        name="weight_back",
    )(
        *hidden,
        first_part[0],
        last_part[0],
        first_part[1],
        last_part[1],
        first_part[2],
        last_part[2],
        *sums,
        bias_sum,
    )


def add_kernel(left, right, later, out):
    out[...] = (left[...].astype(F32) + right[...].astype(F32)).astype(out.dtype)


def add_rows(left, right, later):
    rows, width = left.shape
    block = pl.BlockSpec((rows // 4, width), lambda n: (n, 0))
    return pl.pallas_call(
        add_kernel,
        grid=(4,),
        in_specs=[block, block, ANY],
        out_specs=block,
        out_shape=jax.ShapeDtypeStruct(left.shape, left.dtype),
        compiler_params=limit("add_rows"),
        cost_estimate=cost("add_rows"),
        name="add_rows",
    )(left, right, later)


def unpack_kernel(parts, *refs):
    own, got, outs = refs[0], refs[1 : 1 + parts], refs[1 + parts : -2]
    total, stage = refs[-2:]
    rows, width = outs[0].shape
    result = own[...]
    for item in got:
        result = result + item[...].astype(F32)
    total[...] = result
    outs[0][...] = total[:, :width]
    for pair in range(width // PAIR):
        cols = slice(pair * PAIR, (pair + 1) * PAIR)
        for which in range(2):
            at = width + (2 * pair + which) * PAIR
            outs[1 + which][:, cols] = total[:, at : at + PAIR]
    stage[...] = jnp.zeros_like(stage)
    stage[0:rows, :] = total[:, 3 * width : 3 * width + 128]
    count = outs[-1].shape[0]
    outs[-1][...] = stage[0:1, 16 : 16 + count].reshape(count)
    stage[...] = jnp.transpose(stage[...])
    for n, out in enumerate(outs[3:-1]):
        out[...] = stage[n : n + 1, 0:rows].reshape(rows)


def unpack(own, got, width, count):
    rows = own.shape[0]
    matrix = jax.ShapeDtypeStruct((rows, width), F32)
    vector = jax.ShapeDtypeStruct((rows,), F32)
    return pl.pallas_call(
        functools.partial(unpack_kernel, len(got)),
        in_specs=[VMEM] * (1 + len(got)),
        out_specs=[VMEM] * 12,
        out_shape=[matrix] * 3 + [vector] * 8 + [jax.ShapeDtypeStruct((count,), F32)],
        scratch_shapes=[pltpu.VMEM(own.shape, F32), pltpu.VMEM((128, 128), F32)],
        cost_estimate=pl.CostEstimate(flops=10**9, bytes_accessed=1024, transcendentals=0),
        name="unpack",
    )(own, *got)


def per_device(
    grid,
    hidden_in,
    lengths,
    permutation,
    query_weight,
    query_bias,
    key_weight,
    value_weight,
    value_bias,
    mix_weight,
    mix_bias,
    first_gain,
    first_shift,
    expand_weight,
    expand_bias,
    contract_weight,
    contract_bias,
    second_gain,
    second_shift,
    cotangent,
):
    tokens, width = hidden_in.shape
    wide = contract_weight.shape[0] * grid.devices
    rows = query_weight.shape[0]
    bands = grid.bands

    vectors = [query_bias, value_bias, mix_bias, first_gain, first_shift, contract_bias, second_gain, second_shift]
    weights = [query_weight, key_weight, value_weight, mix_weight, expand_weight, contract_weight]
    shard_a, shard_b, shard_c, doc = pack(lengths, permutation, vectors, expand_bias, weights)

    pieces_a = z_direct(grid, shard_a)
    gather_a = Gather(grid, pieces_a)
    gather_a.near_step()
    pieces_b = z_direct(grid, after(shard_b, *pieces_a))
    pieces_c = z_direct(grid, after(shard_c, *pieces_a, gather_a.near_all))
    gather_b, gather_c = Gather(grid, pieces_b), Gather(grid, pieces_c)
    messages = [hidden_in]
    messages.append(grid.along_z(after(hidden_in, *pieces_b, *pieces_c, gather_a.near_all), 1))
    gather_a.far_step()
    gather_b.near_step()
    messages.append(grid.along_z(messages[1], 1))
    gather_c.near_step()
    parts_a = gather_a.core_step(messages[1])
    gather_b.far_step(messages[1], *gather_a.far_all)
    gather_c.far_step(messages[2])
    parts_b = gather_b.core_step(messages[2])
    for step in range(3, bands):
        messages.append(grid.along_z(messages[-1], 1))
    messages[0] = after(messages[0], gather_c.near_all, gather_b.near_all)

    docs_of = [doc] + [
        item[0:3, 3 * width + 128 :].astype(F32).reshape(1, 3 * 128)[:, :tokens] for item in pieces_a[1:]
    ]
    all_doc = jnp.concatenate(docs_of, axis=1)
    own_doc = doc.reshape(tokens, 1)
    q, kv, attended, logs, vec, b_expand = attend(grid, messages, parts_a, own_doc, all_doc, wide)
    gather_c.far_all = after(gather_c.far_all, attended)
    parts_c = gather_c.core_step()
    result, first, normed, inverse, slope, second, low, keep, send, sums_two = middle(
        grid, attended, hidden_in, cotangent, vec, b_expand, parts_b, parts_c
    )
    sum_c = Sum(grid, keep, send)
    grad_sum, attended_back, keep, send, sums_one, d_b_expand = dense_back(
        grid, attended, first, normed, inverse, slope, second, low, vec, parts_b, parts_c
    )
    sum_b = Sum(grid, keep, send)
    pairs = width // PAIR
    half = pairs // 2
    sum_c.core_step(grad_sum)
    attended_back = after(attended_back, sum_c.send)
    first_part = attend_back(0, half, q, kv, attended_back, attended, logs, own_doc, all_doc)
    sum_c.far_step(first_part)
    sum_b.core_step(sum_c.send)
    attended_back = after(attended_back, sum_b.send, sum_c.send)
    last_part = attend_back(half, pairs - half, q, kv, attended_back, attended, logs, own_doc, all_doc)
    sum_c.near_step(last_part)
    backs = input_back(grid, grad_sum, first_part, last_part, parts_a)
    sent = backs[bands - 1]
    sum_b.far_step(sent)
    d_contract = sum_c.z_step(sent)
    last_part = after(last_part, backs, sum_b.send, d_contract)
    keep, send = weight_back(grid, messages, first_part, last_part, (sums_two, sums_one), d_b_expand)
    sum_a = Sum(grid, keep, send)

    got = grid.along_z(sent, -1)
    sent = add_rows(backs[bands - 2], got, keep)
    sum_a.core_step(sent)
    sum_b.near_step(sum_a.send)
    for piece in range(bands - 2, 0, -1):
        got = grid.along_z(sent, -1)
        if piece == bands - 2:
            sum_a.far_step(sum_b.send)
        if piece > 1:
            sent = add_rows(backs[piece - 1], got, sum_a.send[0])
    sum_a.near_step(sent)
    d_b = sum_b.z_step(sum_a.send)
    grad_input = after(backs[0], d_b) + got.astype(F32)
    sum_a.move_z()
    d_query, d_key, d_value, *small, d_bias = unpack(sum_a.own, sum_a.got, width, expand_bias.shape[0])
    return (
        result,
        grad_input.astype(BF16),
        d_query,
        small[0],
        d_key,
        d_value,
        small[1],
        d_b[:, :width],
        small[2],
        small[3],
        small[4],
        d_b[:, width:],
        d_bias,
        d_contract,
        small[5],
        small[6],
        small[7],
    )


def solution(mesh):
    grid = Grid(mesh.shape["page"], mesh.shape["band"])
    matrix, vector = P(AXES, None), P(AXES)
    parameters = (
        matrix,
        vector,
        matrix,
        matrix,
        vector,
        matrix,
        vector,
        vector,
        vector,
        matrix,
        vector,
        matrix,
        vector,
        vector,
        vector,
    )
    return jax.shard_map(
        functools.partial(per_device, grid),
        mesh=mesh,
        in_specs=(matrix, P("page", None), P("page", "band")) + parameters + (matrix,),
        out_specs=(matrix, matrix) + parameters,
        check_vma=False,
    )
```
